128 devices in a mesh: ty: 8 (over y, core), tx: 16 (over z, x).
Axes of the slice: x: 4, y: 4, z: 4, core: 2. Of those that a mesh axis runs over, the one named last changes fastest.
Arguments:
- object_tiles: float32 [2, 2048, 4096], P(None, 'ty', 'tx'), may hold values from -6 to 6
- previous_tiles: float32 [2, 2048, 4096], P(None, 'ty', 'tx'), may hold values from -6 to 6
- probe_modes: float32 [2, 2, 128, 128], replicated, may hold values from -1.5 to 1.5
- amplitude: float32 [128, 32, 128, 128], P(('ty', 'tx')), may hold values from 0.1 to 13.5
- row_tops: int32 [128], replicated, may hold values from 0 to 128
- scan_cols: int32 [128, 32], P(('ty', 'tx')), may hold values from 0 to 3968, as said below
- restart: int32 [2], replicated, may hold values from 1 to 100, as said below
- owner_map: int32 [8, 16], replicated, may hold values from 0 to 15, each once within a row
Outputs:
- object_out: float32 [2, 2048, 4096], P(None, 'ty', 'tx')
- losses: float32 [2], replicated
The draws below stay inside these ranges and needn't reach their ends.
Inputs may be any that keep to these rules, and one draw needn't show every extreme that they name: `scan_cols`: position j's left column lies in j * 128 to (j + 1) * 128 - 1. `restart`: the counters of the iterations differ from one another. `owner_map`: each row of the map names every tile column once.
All inputs are finite; a program needn't handle non-finite values.
Results may differ from the reference program's by a relative error of at most 0.0003.
Values sent between devices are 32-bit elements; how exact they have to be, the bound alone decides.
No kernel may reach another device: no remote copies, remote signals or barrier semaphores. Data moves between devices by JAX's collectives and lax.ppermute only.
A program may use at most 128 MiB of HBM per device.

```python
import jax
import jax.numpy as jnp
from jax import lax

P_SIZE = 128
MODES = 2
TILE_R = 256
TILE_C = 256
PPT = 2
ITERS = 2
START = 100
BANDS = 8
TILE_COLS = 16
NY = 2048
NX = 4096
NROWS = 128
POS = 32
N_TY = 8
N_TX = 16


def draw_scan_cols(key, part):
    key = jax.random.fold_in(key, 11)
    spacing = TILE_C // PPT
    jitter = jax.random.randint(key, (NROWS, POS), 0, spacing, dtype=jnp.int32)
    base_value = jnp.arange(POS, dtype=jnp.int32) * spacing
    return jnp.minimum(base_value[None, :] + jitter, NX - P_SIZE)


def draw_amplitude(key, part):
    key = jax.random.fold_in(key, 12)
    draw_shape = (NROWS, POS, P_SIZE, P_SIZE)
    row_level = jnp.arange(NROWS, dtype=jnp.float32) / max(NROWS - 1, 1)
    base_value = jax.random.uniform(key, draw_shape, jnp.float32, 0.2, 1.2)
    row_rise = jnp.power(3.0, row_level)
    return base_value * row_rise[:, None, None, None]


def draw_restart(key, part):
    key = jax.random.fold_in(key, 13)
    first_key, second_key = jax.random.split(key)
    top_place = jax.random.randint(first_key, (), 0, ITERS, dtype=jnp.int32)
    others = jax.random.permutation(second_key, START - 1).astype(jnp.int32) + 1
    slots = jnp.arange(ITERS, dtype=jnp.int32)
    shifted = jnp.where(slots > top_place, slots - 1, slots)
    picked = others[jnp.minimum(shifted, START - 2)]
    return jnp.where(slots == top_place, jnp.int32(START), picked)


def place_ends(entries, stream_key, smallest, high):
    spot = [jax.random.randint(jax.random.fold_in(stream_key, axis), (), 0, length) for axis, length in enumerate(entries.shape)]
    main_axis = entries.shape.index(max(entries.shape))
    neighbour = spot[:main_axis] + [(spot[main_axis] + 1) % entries.shape[main_axis]] + spot[main_axis + 1:]
    return entries.at[tuple(spot)].set(smallest).at[tuple(neighbour)].set(high)


def block_scale(key, extent, pieces, smallest, high):
    def one(axis_at, parts):
        steps = jax.random.uniform(jax.random.fold_in(jax.random.fold_in(key, 6), axis_at), (parts,), jnp.float32, smallest / len(pieces), high / len(pieces))
        return jnp.repeat(jnp.exp(steps), extent[axis_at] // parts).reshape((-1,) + (1,) * (len(extent) - axis_at - 1))

    gain = one(*pieces[0])
    for cut in pieces[1:]:
        gain = gain * one(*cut)
    return gain


def bell_draw(stream_key, dims, scale, most, cuts=(), kind=jnp.bfloat16):
    array = jax.random.normal(stream_key, dims, jnp.float32) * scale
    if len(cuts) > 0:
        array = block_scale(stream_key, dims, cuts, -0.22, 0.18) * array
    return jnp.clip(array, min=-most, max=most).astype(kind)


def setup_inputs(seed: int = 0) -> dict:
    splits = jax.random.split(jax.random.key(seed), 9)
    object_tiles = bell_draw(splits[0], (2, NY, NX), 1.0, 6.0, ((1, 8), (2, 16)), jnp.float32)
    previous_tiles = bell_draw(splits[1], (2, NY, NX), 1.0, 6.0, ((1, 8), (2, 16)), jnp.float32)
    probe_modes = bell_draw(splits[2], (MODES, 2, P_SIZE, P_SIZE), 0.25, 1.5, (), jnp.float32)
    amplitude = draw_amplitude(jax.random.fold_in(splits[8], 71), 0)
    row_tops = place_ends(jax.random.randint(splits[4], (NROWS,), 0, TILE_R - P_SIZE + 1), jax.random.fold_in(splits[4], 1), 0, TILE_R - P_SIZE).astype(jnp.int32)
    scan_cols = draw_scan_cols(jax.random.fold_in(splits[8], 71), 0)
    restart = draw_restart(jax.random.fold_in(splits[8], 71), 0)
    owner_map = jax.vmap(lambda own: jax.random.permutation(own, N_TX))(jax.random.split(splits[7], BANDS)).reshape((BANDS, TILE_COLS)).astype(jnp.int32)
    return {"object_tiles": object_tiles, "previous_tiles": previous_tiles, "probe_modes": probe_modes, "amplitude": amplitude, "row_tops": row_tops, "scan_cols": scan_cols, "restart": restart, "owner_map": owner_map}


stabilizer = 0.05
step_length = 0.25

def momentum_table():
    values = [1.0]
    for counter in range(START):
        previous_value = values[-1]
        values.append((1.0 + (1.0 + 4.0 * previous_value * previous_value) ** 0.5) / 2.0)
    return jnp.asarray(values, jnp.float32)

def to_logical(stored, owner_map):
    blocks = stored.reshape(2, N_TY, TILE_R, N_TX, TILE_C)
    picked = jax.vmap(lambda part_blocks, column_order: jnp.take(part_blocks, column_order, axis=2), in_axes=(1, 0), out_axes=1)(blocks, owner_map)
    return picked.reshape(2, N_TY * TILE_R, N_TX * TILE_C)

def to_stored(logical, owner_map):
    blocks = logical.reshape(2, N_TY, TILE_R, N_TX, TILE_C)
    inverse = jnp.argsort(owner_map, axis=1).astype(jnp.int32)
    picked = jax.vmap(lambda part_blocks, column_order: jnp.take(part_blocks, column_order, axis=2), in_axes=(1, 0), out_axes=1)(blocks, inverse)
    return picked.reshape(2, N_TY * TILE_R, N_TX * TILE_C)

def row_pass(extrapolated, probe_modes, amplitude, row_tops, scan_cols):
    field = lax.complex(extrapolated[0], extrapolated[1])
    probe_wave = lax.complex(probe_modes[:, 0], probe_modes[:, 1])

    def one_row(running, row_data):
        gradient, total_loss = running
        scan_row, offsets, measured = row_data
        row_top = scan_row // N_TX * TILE_R + row_tops[scan_row]
        patch_strip = lax.dynamic_slice(field, (row_top, jnp.int32(0)), (P_SIZE, N_TX * TILE_C))
        patches = jax.vmap(lambda col_start: lax.dynamic_slice(patch_strip, (jnp.int32(0), col_start), (P_SIZE, P_SIZE)))(offsets)
        waves = jnp.fft.fft2(probe_wave[None] * patches[:, None], norm='ortho')
        magnitude = jnp.sqrt(lax.optimization_barrier(jnp.sum(jnp.real(waves) ** 2 + jnp.imag(waves) ** 2, axis=1)) + stabilizer)
        total_loss = total_loss + 0.5 * jnp.sum((magnitude - measured) ** 2)
        weight = 1.0 - measured / magnitude
        back_waves = jnp.fft.ifft2(weight[:, None] * waves, norm='ortho')
        patch_grads = lax.optimization_barrier(jnp.sum(jnp.conj(probe_wave)[None] * back_waves, axis=1))

        def place(position, accumulated):
            col_start = offsets[position]
            previous_sum = lax.dynamic_slice(accumulated, (jnp.int32(0), col_start), (P_SIZE, P_SIZE))
            return lax.dynamic_update_slice(accumulated, previous_sum + patch_grads[position], (jnp.int32(0), col_start))
        strip_grad = lax.fori_loop(0, offsets.shape[0], place, jnp.zeros((P_SIZE, N_TX * TILE_C), field.dtype))
        previous_rows = lax.dynamic_slice(gradient, (row_top, jnp.int32(0)), (P_SIZE, N_TX * TILE_C))
        gradient = lax.dynamic_update_slice(gradient, previous_rows + strip_grad, (row_top, jnp.int32(0)))
        return ((gradient, total_loss), None)
    row_ids = jnp.arange(N_TY * N_TX, dtype=jnp.int32)
    start_state = (jnp.zeros(field.shape, field.dtype), jnp.zeros((), extrapolated.dtype))
    (gradient, total_loss), unused = lax.scan(one_row, start_state, (row_ids, scan_cols, amplitude))
    return (jnp.stack([jnp.real(gradient), jnp.imag(gradient)]), total_loss)

def reference(object_tiles, previous_tiles, probe_modes, amplitude, row_tops, scan_cols, restart, owner_map):
    table = momentum_table()
    current = to_logical(object_tiles, owner_map)
    before = to_logical(previous_tiles, owner_map)
    loss_list = []
    for iteration in range(ITERS):
        counter = restart[iteration]
        momentum = (table[counter - 1] - 1.0) / table[counter]
        extrapolated = current + momentum * (current - before)
        gradient, total_loss = row_pass(extrapolated, probe_modes, amplitude, row_tops, scan_cols)
        loss_list.append(total_loss / (N_TY * N_TX * POS * P_SIZE * P_SIZE))
        before = current
        current = extrapolated - step_length * gradient
    return (to_stored(current, owner_map), jnp.stack(loss_list))
```

```python
import functools
import math

import jax
import jax.numpy as jnp
import ml_dtypes
import numpy as np
from jax import lax
from jax.experimental import pallas as pl
from jax.experimental.pallas import tpu as pltpu
from jax.sharding import PartitionSpec as P

START = 100
STABILIZER = 0.05
STEP = 0.25
N = 128
GROUP = 4
f32 = jnp.float32
bf16 = jnp.bfloat16
SMEM = pl.BlockSpec(memory_space=pltpu.SMEM)
VMEM = pl.BlockSpec(memory_space=pltpu.VMEM)
ANY = pl.BlockSpec(memory_space=pl.ANY)


def momentum_table():
    values = [1.0]
    for counter in range(START):
        last = values[-1]
        values.append((1.0 + (1.0 + 4.0 * last * last) ** 0.5) / 2.0)
    return jnp.asarray(values, f32)


def dft_tables():
    index = np.arange(N)
    angle = (index[:, None] * index[None, :] % N).astype(np.float64) * (2.0 * math.pi / N)
    cos, sin = np.cos(angle) / math.sqrt(N), np.sin(angle) / math.sqrt(N)

    def stacked(table):
        high = table.astype(ml_dtypes.bfloat16)
        low = (table - high.astype(np.float64)).astype(ml_dtypes.bfloat16)
        return jnp.asarray(np.concatenate([high, high, low], 0))

    return stacked(np.block([[cos, -sin], [sin, cos]])), stacked(np.block([[cos, sin], [-sin, cos]]))


def times_table(block, table):
    high = block.astype(bf16)
    low = (block - high.astype(f32)).astype(bf16)
    return jnp.dot(jnp.concatenate([high, low, high], 1), table, preferred_element_type=f32)


def flip_blocks(block):
    rows = []
    for at in range(0, block.shape[0], N):
        rows.append(jnp.concatenate([block[at : at + N, :N].T, block[at : at + N, N:].T], 1))
    return jnp.concatenate(rows, 0)


def add_positions(rows, offs, z, probe, amp, fwd, bwd, low, high, loss):
    lane = lax.broadcasted_iota(jnp.int32, (N, N), 1)
    first = pl.program_id(0) * GROUP
    waves, places = [], []
    for u in range(GROUP):
        top, off = rows[first + u], offs[first + u]
        inside = lane >= off
        patch = [
            pltpu.roll(jnp.where(inside, z[0, k, pl.ds(top, N), :], z[1, k, pl.ds(top, N), :]), (N - off) & (N - 1), 1)
            for k in range(2)
        ]
        for m in range(2):
            re, im = probe[m, 0], probe[m, 1]
            waves.append(jnp.concatenate([re * patch[0] - im * patch[1], re * patch[1] + im * patch[0]], 1))
        places.append((top, off, inside))
    wave = times_table(flip_blocks(times_table(jnp.concatenate(waves, 0), fwd[...])), fwd[...])
    backs = []
    total = jnp.zeros((8, N), f32)
    for u in range(GROUP):
        w = wave[u * 2 * N : (u + 1) * 2 * N]
        square = w * w
        square = square[:N] + square[N:]
        square = square[:, :N] + square[:, N:] + STABILIZER
        inverse = lax.rsqrt(square)
        measured = amp[u].T
        miss = square * inverse - measured
        total = total + jnp.sum((miss * miss).reshape(N // 8, 8, N), 0)
        weight = 1.0 - measured * inverse
        weight = jnp.concatenate([weight, weight], 1)
        backs += [weight * w[:N], weight * w[N:]]
    loss[...] += total
    back = times_table(flip_blocks(times_table(jnp.concatenate(backs, 0), bwd[...])), bwd[...])
    for u, (top, off, inside) in enumerate(places):
        grad_re, grad_im = 0.0, 0.0
        for m in range(2):
            re, im = probe[m, 0], probe[m, 1]
            b = back[(2 * u + m) * N : (2 * u + m + 1) * N]
            grad_re = grad_re + re * b[:, :N] + im * b[:, N:]
            grad_im = grad_im + re * b[:, N:] - im * b[:, :N]
        for k, grad in ((0, grad_re), (1, grad_im)):
            moved = pltpu.roll(grad, off, 1)
            low[k, pl.ds(top, N), :] += jnp.where(inside, moved, 0.0)
            high[k, pl.ds(top, N), :] += jnp.where(inside, 0.0, moved)


def clear(*refs):
    for ref in refs:
        ref[...] = jnp.zeros_like(ref)


def unit(tile, k, u):
    return tile[k, :, u * N : (u + 1) * N]


def even_first(rows, offs, beta, z0, obj, probe, amp, fwd, bwd, low, high, ahead, loss):
    @pl.when(pl.program_id(0) == 0)
    def _():
        clear(low, high, loss)

    add_positions(rows, offs, z0, probe, amp, fwd, bwd, low, high, loss)

    @pl.when(pl.program_id(0) == pl.num_programs(0) - 1)
    def _():
        b = beta[1]
        for k in range(2):
            ahead[k] = (1.0 + b) * (z0[0, k] - STEP * low[k]) - b * unit(obj, k, 0)


def odd_first(rows, offs, z0, halo, probe, amp, fwd, bwd, low, high, loss, z):
    @pl.when(pl.program_id(0) == 0)
    def _():
        clear(low, high, loss)
        z[0] = z0[1]
        z[1] = halo[...]

    add_positions(rows, offs, z, probe, amp, fwd, bwd, low, high, loss)


def odd_second(rows, offs, beta, z0, obj, even_high, odd_low, odd_high, ahead, probe, amp, fwd, bwd, low, high, loss, z):
    @pl.when(pl.program_id(0) == 0)
    def _():
        clear(low, high, loss)
        b = beta[1]
        for k in range(2):
            now = z0[1, k] - STEP * (even_high[k] + odd_low[k])
            z[0, k] = now + b * (now - unit(obj, k, 1))
            z[1, k] = ahead[k] - ((1.0 + b) * STEP) * odd_high[k]

    add_positions(rows, offs, z, probe, amp, fwd, bwd, low, high, loss)


def even_second(
    rows, offs, beta, z0, obj, even_low, even_high, odd_low, left, odd_low_second, loss_a, loss_b, loss_c,
    probe, amp, fwd, bwd, tile, sums, low, high, loss, z,
):
    @pl.when(pl.program_id(0) == 0)
    def _():
        clear(low, high, loss)
        b = beta[1]
        for k in range(2):
            now = z0[0, k] - STEP * (even_low[k] + left[k])
            z[0, k] = now + b * (now - unit(obj, k, 0))
            now = z0[1, k] - STEP * (even_high[k] + odd_low[k])
            z[1, k] = now + b * (now - unit(obj, k, 1))

    add_positions(rows, offs, z, probe, amp, fwd, bwd, low, high, loss)

    @pl.when(pl.program_id(0) == pl.num_programs(0) - 1)
    def _():
        for k in range(2):
            tile[k, :, :N] = z[0, k] - STEP * low[k]
            tile[k, :, N:] = z[1, k] - STEP * (high[k] + odd_low_second[k])
        before = jnp.sum(loss_a[...] + loss_b[...], axis=0, keepdims=True)
        after = jnp.sum(loss_c[...] + loss[...], axis=0, keepdims=True)
        lane = lax.broadcasted_iota(jnp.int32, (1, N), 1)
        line = jnp.where(lane < N // 2, before + pltpu.roll(before, N // 2, 1), after + pltpu.roll(after, N // 2, 1))
        sums[...] = jnp.broadcast_to(line, sums.shape)


def run(kernel, count, smalls, blocks, probe, amp, tables, outs, scratch):
    shape = lambda s: jax.ShapeDtypeStruct(s, f32)
    whole = lambda a: pl.BlockSpec(a.shape, lambda i, n=len(a.shape): (0,) * n)
    out_shape = [shape(s) for s in outs]
    return pl.pallas_call(
        kernel,
        grid=(count // GROUP,),
        out_shape=out_shape,
        in_specs=[SMEM] * len(smalls)
        + [whole(b) for b in blocks]
        + [whole(probe), pl.BlockSpec((GROUP, N, N), lambda i: (i, 0, 0))]
        + [whole(t) for t in tables],
        out_specs=[whole(o) for o in out_shape],
        scratch_shapes=scratch,
        compiler_params=pltpu.CompilerParams(vmem_limit_bytes=40 * 2**20),
        cost_estimate=pl.CostEstimate(flops=count * 400_000_000, bytes_accessed=2**22, transcendentals=count * N * N),
    )(*smalls, *blocks, probe, amp, *tables)


def prepare(inv, cols, beta, obj, prev, amp, z0, send_even, send_odd, chunk, places, sems):
    copies = []

    def copy(source, target):
        c = pltpu.make_async_copy(source, target, sems.at[len(copies)])
        c.start()
        copies.append(c)

    for d in range(16):
        col = inv[d]
        copy(amp.at[2 * col], send_even.at[d, pl.ds(0, N)])
        copy(amp.at[2 * col + 1], send_odd.at[d])
    b = beta[0]
    for u in range(2):
        for k in range(2):
            now = unit(obj, k, u)
            z0[u, k] = now + b * (now - unit(prev, k, u))
    lane = lax.broadcasted_iota(jnp.int32, (8, N), 1)
    for d in range(16):
        col = inv[d]
        even = cols[2 * col] - 2 * N * col
        odd = cols[2 * col + 1] - 2 * N * col - N
        places[d] = jnp.where(lane < N // 2, even, odd).astype(f32)
        chunk[d] = z0[0, d // 8, pl.ds(32 * (d % 8), 32), :]
    for d in range(16):
        copy(chunk.at[d], send_even.at[d, pl.ds(N, 32)])
        copy(places.at[d], send_even.at[d, pl.ds(N + 32, 8)])
    for c in copies:
        c.wait()


def pick(source, got, sent):
    for d in range(16):
        sent[d] = got[source[d]]


def pick_chunks(got, source, at):
    return pl.pallas_call(
        pick,
        grid=(1,),
        out_shape=jax.ShapeDtypeStruct((16, 32, N), f32),
        in_specs=[SMEM, pl.BlockSpec((16, 32, N), lambda i: (0, at, 0))],
        out_specs=pl.BlockSpec((16, 32, N), lambda i: (0, 0, 0)),
        compiler_params=pltpu.CompilerParams(vmem_limit_bytes=4 * 2**20),
    )(source, got)


def swap(block):
    return lax.all_to_all(block, "tx", 0, 0, tiled=True)


def shards(obj, prev, probe, amplitude, row_tops, scan_cols, restart, owner_map):
    band = lax.axis_index("ty")
    owner = owner_map[band]
    columns = jnp.arange(16, dtype=jnp.int32)
    inv = jnp.sum(jnp.where(owner[None, :] == columns[:, None], columns[None, :], 0), axis=1)
    hot = lambda want: jnp.sum(jnp.where(want[:, None] == columns[None, :], owner[None, :], 0), axis=1)
    from_right = hot((inv + 1) % 16)
    from_left = hot((inv + 15) % 16)
    rows = lax.dynamic_slice(row_tops, (band * 16,), (16,))
    table = momentum_table()
    beta = (table[restart - 1] - 1.0) / table[restart]
    tables = dft_tables()
    unit_shape = (2, 256, N)
    z_scratch = [pltpu.VMEM((2, 2, 256, N), f32)]

    z0, send_even, send_odd = pl.pallas_call(
        prepare,
        out_shape=[
            jax.ShapeDtypeStruct((2, 2, 256, N), f32),
            jax.ShapeDtypeStruct((16, N + 40, N), f32),
            jax.ShapeDtypeStruct((16, N, N), f32),
        ],
        in_specs=[SMEM, SMEM, SMEM, VMEM, VMEM, ANY],
        out_specs=[VMEM, ANY, ANY],
        scratch_shapes=[pltpu.VMEM((16, 32, N), f32), pltpu.VMEM((16, 8, N), f32), pltpu.SemaphoreType.DMA((64,))],
        compiler_params=pltpu.CompilerParams(vmem_limit_bytes=8 * 2**20),
    )(inv, scan_cols[0], beta, obj, prev, amplitude[0])

    amp_even = swap(send_even)
    amp_odd = swap(send_odd)
    offs = jnp.round(amp_even[:, N + 32, :]).astype(jnp.int32)
    off_even, off_odd = offs[:, 0], offs[:, N // 2]

    halo = swap(pick_chunks(amp_even, from_right, N // 32)).reshape(unit_shape)
    even_low, even_high, ahead, loss_a = run(
        even_first, 16, [rows, off_even, beta], [z0, obj], probe, amp_even, tables,
        [unit_shape, unit_shape, unit_shape, (8, N)], [],
    )
    ahead = swap(ahead.reshape(16, 32, N))
    odd_low, odd_high, loss_b = run(
        odd_first, 16, [rows, off_odd], [z0, halo], probe, amp_odd, tables, [unit_shape, unit_shape, (8, N)], z_scratch
    )
    ahead = swap(pick_chunks(ahead, from_right, 0)).reshape(unit_shape)
    left = swap(odd_high.reshape(16, 32, N))
    odd_low_second, odd_high_second, loss_c = run(
        odd_second, 16, [rows, off_odd, beta], [z0, obj, even_high, odd_low, odd_high, ahead], probe, amp_odd, tables,
        [unit_shape, unit_shape, (8, N)], z_scratch,
    )
    left = swap(pick_chunks(left, from_left, 0)).reshape(unit_shape)
    last = swap(odd_high_second.reshape(16, 32, N))
    tile, sums = run(
        even_second, 16, [rows, off_even, beta],
        [z0, obj, even_low, even_high, odd_low, left, odd_low_second, loss_a, loss_b, loss_c], probe, amp_even, tables,
        [(2, 256, 256), (N, N)], [pltpu.VMEM(unit_shape, f32), pltpu.VMEM(unit_shape, f32), pltpu.VMEM((8, N), f32)] + z_scratch,
    )
    last = swap(pick_chunks(last, from_left, 0)).reshape(unit_shape)
    tile = tile.at[:, :, :N].add(-STEP * last)
    sums = lax.all_to_all(sums, ("ty", "tx"), 0, 0, tiled=True)
    losses = jnp.sum(jnp.sum(sums, axis=0).reshape(2, N // 2), axis=1) * (0.5 / 67108864.0)
    return (tile, losses)


def solution(mesh):
    in_specs = (
        P(None, "ty", "tx"),
        P(None, "ty", "tx"),
        P(),
        P(("ty", "tx"), None, None, None),
        P(),
        P(("ty", "tx"), None),
        P(),
        P(),
    )
    return jax.shard_map(
        shards, mesh=mesh, in_specs=in_specs, out_specs=(P(None, "ty", "tx"), P()), check_vma=False
    )
```

```python
import functools
import math

import jax
import jax.numpy as jnp
import ml_dtypes
import numpy as np
from jax import lax
from jax.experimental import pallas as pl
from jax.experimental.pallas import tpu as pltpu
from jax.sharding import PartitionSpec as P

START = 100
STABILIZER = 0.05
STEP = 0.25
N = 128
GROUP = 4
VMEM_BYTES = 60 * 2**20
f32 = jnp.float32
bf16 = jnp.bfloat16
SMEM = pl.BlockSpec(memory_space=pltpu.SMEM)
VMEM = pl.BlockSpec(memory_space=pltpu.VMEM)
ANY = pl.BlockSpec(memory_space=pl.ANY)


def momentum_table():
    values = [1.0]
    for counter in range(START):
        last = values[-1]
        values.append((1.0 + (1.0 + 4.0 * last * last) ** 0.5) / 2.0)
    return jnp.asarray(values, f32)


def dft_tables():
    index = np.arange(N)
    angle = (index[:, None] * index[None, :] % N).astype(np.float64) * (2.0 * math.pi / N)
    cos, sin = np.cos(angle) / math.sqrt(N), np.sin(angle) / math.sqrt(N)

    def stacked(table):
        high = table.astype(ml_dtypes.bfloat16)
        low = (table - high.astype(np.float64)).astype(ml_dtypes.bfloat16)
        return jnp.asarray(np.concatenate([high, high, low], 0))

    return stacked(np.block([[cos, -sin], [sin, cos]])), stacked(np.block([[cos, sin], [-sin, cos]]))


def times_table(block, table):
    high = block.astype(bf16)
    low = (block - high.astype(f32)).astype(bf16)
    return jnp.dot(jnp.concatenate([high, low, high], 1), table, preferred_element_type=f32)


def flip_blocks(block):
    rows = []
    for at in range(0, block.shape[0], N):
        rows.append(jnp.concatenate([block[at : at + N, :N].T, block[at : at + N, N:].T], 1))
    return jnp.concatenate(rows, 0)


def add_positions(rows, offs, z, probe, amp, fwd, bwd, low, high, loss):
    lane = lax.broadcasted_iota(jnp.int32, (N, N), 1)
    first = pl.program_id(0) * GROUP
    waves, places = [], []
    for u in range(GROUP):
        top, off = rows[first + u], offs[first + u]
        inside = lane >= off
        patch = [
            pltpu.roll(jnp.where(inside, z[0, k, pl.ds(top, N), :], z[1, k, pl.ds(top, N), :]), (N - off) & (N - 1), 1)
            for k in range(2)
        ]
        for m in range(2):
            re, im = probe[m, 0], probe[m, 1]
            waves.append(jnp.concatenate([re * patch[0] - im * patch[1], re * patch[1] + im * patch[0]], 1))
        places.append((top, off, inside))
    wave = times_table(flip_blocks(times_table(jnp.concatenate(waves, 0), fwd[...])), fwd[...])
    backs = []
    total = jnp.zeros((8, N), f32)
    for u in range(GROUP):
        w = wave[u * 2 * N : (u + 1) * 2 * N]
        square = w * w
        square = square[:N] + square[N:]
        square = square[:, :N] + square[:, N:] + STABILIZER
        inverse = lax.rsqrt(square)
        measured = amp[u].T
        miss = square * inverse - measured
        total = total + jnp.sum((miss * miss).reshape(N // 8, 8, N), 0)
        weight = 1.0 - measured * inverse
        weight = jnp.concatenate([weight, weight], 1)
        backs += [weight * w[:N], weight * w[N:]]
    loss[...] += total
    back = times_table(flip_blocks(times_table(jnp.concatenate(backs, 0), bwd[...])), bwd[...])
    for u, (top, off, inside) in enumerate(places):
        grad_re, grad_im = 0.0, 0.0
        for m in range(2):
            re, im = probe[m, 0], probe[m, 1]
            b = back[(2 * u + m) * N : (2 * u + m + 1) * N]
            grad_re = grad_re + re * b[:, :N] + im * b[:, N:]
            grad_im = grad_im + re * b[:, N:] - im * b[:, :N]
        for k, grad in ((0, grad_re), (1, grad_im)):
            moved = pltpu.roll(grad, off, 1)
            low[k, pl.ds(top, N), :] += jnp.where(inside, moved, 0.0)
            high[k, pl.ds(top, N), :] += jnp.where(inside, 0.0, moved)


def clear(*refs):
    for ref in refs:
        ref[...] = jnp.zeros_like(ref)


def unit(tile, k, u):
    return tile[k, :, u * N : (u + 1) * N]


def chunk_of(ref, d):
    return ref.at[d // 8, pl.ds(32 * (d % 8), 32)]


def even_first(rows, offs, beta, z0, obj, probe, amp, fwd, bwd, low, high, ahead, loss):
    @pl.when(pl.program_id(0) == 0)
    def _():
        clear(low, high, loss)

    add_positions(rows, offs, z0, probe, amp, fwd, bwd, low, high, loss)

    @pl.when(pl.program_id(0) == pl.num_programs(0) - 1)
    def _():
        b = beta[1]
        for k in range(2):
            ahead[k] = (1.0 + b) * (z0[0, k] - STEP * low[k]) - b * unit(obj, k, 0)


def odd_first(rows, offs, beta, z0, obj, even_high, ahead, halo, probe, amp, fwd, bwd, mid, send, loss, low, high, z):
    @pl.when(pl.program_id(0) == 0)
    def _():
        clear(low, high, loss)
        z[0] = z0[1]
        for d in range(16):
            chunk_of(z.at[1], d)[...] = halo[d]

    add_positions(rows, offs, z, probe, amp, fwd, bwd, low, high, loss)

    @pl.when(pl.program_id(0) == pl.num_programs(0) - 1)
    def _():
        b = beta[1]
        for k in range(2):
            now = z0[1, k] - STEP * (even_high[k] + low[k])
            mid[k] = now + b * (now - unit(obj, k, 1))
        for d in range(16):
            send[d, :32] = chunk_of(ahead, d)[...]
            send[d, 32:] = chunk_of(high, d)[...]


def odd_second(rows, offs, mid, got, probe, amp, fwd, bwd, low, high, loss, z):
    @pl.when(pl.program_id(0) == 0)
    def _():
        clear(low, high, loss)
        z[0] = mid[...]
        for d in range(16):
            chunk_of(z.at[1], d)[...] = got[d, 32:]

    add_positions(rows, offs, z, probe, amp, fwd, bwd, low, high, loss)


def even_second(
    rows, offs, mid, got, odd_low, loss_a, loss_b, loss_c, probe, amp, fwd, bwd, tile, sums, low, high, loss, z
):
    @pl.when(pl.program_id(0) == 0)
    def _():
        clear(low, high, loss)
        z[1] = mid[...]
        for d in range(16):
            chunk_of(z.at[0], d)[...] = got[d, :32]

    add_positions(rows, offs, z, probe, amp, fwd, bwd, low, high, loss)

    @pl.when(pl.program_id(0) == pl.num_programs(0) - 1)
    def _():
        for k in range(2):
            tile[k, :, :N] = z[0, k] - STEP * low[k]
            tile[k, :, N:] = z[1, k] - STEP * (high[k] + odd_low[k])
        before = jnp.sum(loss_a[...] + loss_b[...], axis=0, keepdims=True)
        after = jnp.sum(loss_c[...] + loss[...], axis=0, keepdims=True)
        lane = lax.broadcasted_iota(jnp.int32, (1, N), 1)
        line = jnp.where(lane < N // 2, before + pltpu.roll(before, N // 2, 1), after + pltpu.roll(after, N // 2, 1))
        sums[...] = jnp.broadcast_to(line, sums.shape)


def run(kernel, count, smalls, blocks, probe, amp, tables, outs, scratch):
    shape = lambda s: jax.ShapeDtypeStruct(s, f32)
    whole = lambda a: pl.BlockSpec(a.shape, lambda i, n=len(a.shape): (0,) * n)
    out_shape = [shape(s) for s in outs]
    return pl.pallas_call(
        kernel,
        grid=(count // GROUP,),
        out_shape=out_shape,
        in_specs=[SMEM] * len(smalls)
        + [spec or whole(b) for b, spec in blocks]
        + [whole(probe), pl.BlockSpec((GROUP, N, N), lambda i: (i, 0, 0))]
        + [whole(t) for t in tables],
        out_specs=[whole(o) for o in out_shape],
        scratch_shapes=scratch,
        compiler_params=pltpu.CompilerParams(vmem_limit_bytes=VMEM_BYTES),
        cost_estimate=pl.CostEstimate(flops=count * 400_000_000, bytes_accessed=2**22, transcendentals=count * N * N),
    )(*smalls, *[b for b, _ in blocks], probe, amp, *tables)


def small_call(kernel, args, outs, scratch=()):
    return pl.pallas_call(
        kernel,
        out_shape=[jax.ShapeDtypeStruct(s, d) for s, d, _ in outs],
        in_specs=[spec for _, spec in args],
        out_specs=[spec for _, _, spec in outs],
        scratch_shapes=list(scratch),
        compiler_params=pltpu.CompilerParams(vmem_limit_bytes=VMEM_BYTES),
    )(*[a for a, _ in args])


def start_all(pairs, sems):
    copies = [pltpu.make_async_copy(a, b, sems.at[i]) for i, (a, b) in enumerate(pairs)]
    for c in copies:
        c.start()
    return copies


def prepare(
    owner_map, row_tops, restart, table, cols, obj, prev, amp,
    z0, send, rows, inv, right, left, beta, sems,
):
    band = lax.axis_index("ty")
    for c in range(16):
        owner = owner_map[band, c]
        inv[owner] = c
        right[owner] = owner_map[band, (c + 1) % 16]
        left[owner] = owner_map[band, (c + 15) % 16]
        rows[c] = row_tops[band * 16 + c]
    copies = start_all([(amp.at[2 * inv[d]], send.at[d, pl.ds(0, N)]) for d in range(16)], sems)
    for k in range(2):
        beta[k] = (table[restart[k] - 1] - 1.0) / table[restart[k]]
    b = beta[0]
    for u in range(2):
        for k in range(2):
            now = unit(obj, k, u)
            z0[u, k] = now + b * (now - unit(prev, k, u))
    lane = lax.broadcasted_iota(jnp.int32, (8, N), 1)
    for d in range(16):
        col = inv[d]
        even = cols[0, 2 * col] - 2 * N * col
        odd = cols[0, 2 * col + 1] - 2 * N * col - N
        send[d, N : N + 32] = chunk_of(z0.at[0], d)[...]
        send[d, N + 32 :] = jnp.where(lane < N // 2, even, odd).astype(f32)
    for c in copies:
        c.wait()


def pass_halo(right, inv, got, amp, send, sems, more_sems):
    copies = start_all([(amp.at[2 * inv[d] + 1], send.at[d, pl.ds(0, N)]) for d in range(16)], sems)
    copies += start_all([(got.at[right[d], pl.ds(N, 32)], send.at[d, pl.ds(N, 32)]) for d in range(16)], more_sems)
    for c in copies:
        c.wait()


def join(left, right, beta, got, send, total):
    scale = (1.0 + beta[1]) * STEP
    for d in range(16):
        total[d] = got[d, :32] - scale * got[left[d], 32:]
    for d in range(16):
        send[d, :32] = total[d]
        send[d, 32:] = total[right[d]]


def pass_last(left, got, sums, send):
    for d in range(16):
        send[d, :32] = got[left[d]]
        send[d, 32:] = sums[...]


def finish(tile, got, out, sums):
    total = got[0, 32:]
    for d in range(1, 16):
        total = total + got[d, 32:]
    sums[...] = total
    for k in range(2):
        out[k, :, N:] = tile[k, :, N:]
    for d in range(16):
        at = pl.ds(32 * (d % 8), 32)
        out[d // 8, at, :N] = tile[d // 8, at, :N] - STEP * got[d, :32]


def swap(block, axis="tx"):
    return lax.all_to_all(block, axis, 0, 0, tiled=True)


def shards(obj, prev, probe, amplitude, row_tops, scan_cols, restart, owner_map):
    tables = dft_tables()
    unit_shape = (2, 256, N)
    unit_vmem = pltpu.VMEM(unit_shape, f32)
    z_vmem = pltpu.VMEM((2,) + unit_shape, f32)
    ints = ((16,), jnp.int32, SMEM)

    z0, send, rows, inv, right, left, beta = small_call(
        prepare,
        [(owner_map, SMEM), (row_tops, SMEM), (restart, SMEM), (momentum_table(), SMEM), (scan_cols, SMEM),
         (obj, VMEM), (prev, VMEM), (amplitude[0], ANY)],
        [((2,) + unit_shape, f32, VMEM), ((16, N + 40, N), f32, VMEM), ints, ints, ints, ints, ((2,), f32, SMEM)],
        [pltpu.SemaphoreType.DMA((16,))],
    )
    amp_even = swap(send)
    (send,) = small_call(
        pass_halo,
        [(right, SMEM), (inv, SMEM), (amp_even, ANY), (amplitude[0], ANY)],
        [((16, N + 32, N), f32, VMEM)],
        [pltpu.SemaphoreType.DMA((16,)), pltpu.SemaphoreType.DMA((16,))],
    )
    amp_odd = swap(send)
    offs = jnp.round(amp_even[:, N + 32, :]).astype(jnp.int32)
    off_even, off_odd = offs[:, 0], offs[:, N // 2]

    even_low, even_high, ahead, loss_a = run(
        even_first, 16, [rows, off_even, beta], [(z0, None), (obj, None)], probe, amp_even, tables,
        [unit_shape, unit_shape, unit_shape, (8, N)], [],
    )
    mid, send, loss_b = run(
        odd_first, 16, [rows, off_odd, beta],
        [(z0, None), (obj, None), (even_high, None), (ahead, None),
         (amp_odd, pl.BlockSpec((16, 32, N), lambda i: (0, N // 32, 0)))],
        probe, amp_odd, tables, [unit_shape, (16, 64, N), (8, N)], [unit_vmem, unit_vmem, z_vmem],
    )
    got = swap(send)
    (send,) = small_call(
        join, [(left, SMEM), (right, SMEM), (beta, SMEM), (got, VMEM)], [((16, 64, N), f32, VMEM)],
        [pltpu.VMEM((16, 32, N), f32)],
    )
    got = swap(send)
    odd_low, odd_high, loss_c = run(
        odd_second, 16, [rows, off_odd], [(mid, None), (got, None)], probe, amp_odd, tables,
        [unit_shape, unit_shape, (8, N)], [z_vmem],
    )
    last = swap(odd_high.reshape(16, 32, N))
    tile, sums = run(
        even_second, 16, [rows, off_even],
        [(x, None) for x in (mid, got, odd_low, loss_a, loss_b, loss_c)], probe, amp_even, tables,
        [(2, 256, 256), (8, N)], [unit_vmem, unit_vmem, pltpu.VMEM((8, N), f32), z_vmem],
    )
    (send,) = small_call(
        pass_last, [(left, SMEM), (last, VMEM), (sums, VMEM)], [((16, 40, N), f32, VMEM)]
    )
    got = swap(send)
    tile, sums = small_call(
        finish, [(tile, VMEM), (got, VMEM)], [((2, 256, 256), f32, VMEM), ((8, N), f32, VMEM)]
    )
    sums = swap(sums, "ty")
    losses = jnp.sum(jnp.sum(sums, axis=0).reshape(2, N // 2), axis=1) * (0.5 / 67108864.0)
    return (tile, losses)


def solution(mesh):
    in_specs = (
        P(None, "ty", "tx"),
        P(None, "ty", "tx"),
        P(),
        P(("ty", "tx"), None, None, None),
        P(),
        P(("ty", "tx"), None),
        P(),
        P(),
    )
    return jax.shard_map(
        shards, mesh=mesh, in_specs=in_specs, out_specs=(P(None, "ty", "tx"), P()), check_vma=False
    )
```

```python
import functools
import math

import jax
import jax.numpy as jnp
import ml_dtypes
import numpy as np
from jax import lax
from jax.experimental import pallas as pl
from jax.experimental.pallas import tpu as pltpu
from jax.sharding import PartitionSpec as P

START = 100
STABILIZER = 0.05
STEP = 0.25
N = 128
GROUP = 8
VMEM_BYTES = 60 * 2**20
f32 = jnp.float32
bf16 = jnp.bfloat16
SMEM = pl.BlockSpec(memory_space=pltpu.SMEM)
VMEM = pl.BlockSpec(memory_space=pltpu.VMEM)
ANY = pl.BlockSpec(memory_space=pl.ANY)


def momentum_table():
    values = [1.0]
    for counter in range(START):
        last = values[-1]
        values.append((1.0 + (1.0 + 4.0 * last * last) ** 0.5) / 2.0)
    return jnp.asarray(values, f32)


def dft_tables():
    index = np.arange(N)
    angle = (index[:, None] * index[None, :] % N).astype(np.float64) * (2.0 * math.pi / N)
    cos, sin = np.cos(angle) / math.sqrt(N), np.sin(angle) / math.sqrt(N)

    def stacked(table):
        high = table.astype(ml_dtypes.bfloat16)
        low = (table - high.astype(np.float64)).astype(ml_dtypes.bfloat16)
        return jnp.asarray(np.concatenate([high, high, low], 0))

    return stacked(np.block([[cos, -sin], [sin, cos]])), stacked(np.block([[cos, sin], [-sin, cos]]))


def times_table(block, table):
    parts = []
    for at in range(0, block.shape[0], N):
        part = block[at : at + N]
        high = part.astype(bf16)
        low = (part - high.astype(f32)).astype(bf16)
        parts.append(jnp.dot(jnp.concatenate([high, low, high], 1), table, preferred_element_type=f32))
    return jnp.concatenate(parts, 0)


def flip_blocks(block):
    rows = []
    for at in range(0, block.shape[0], N):
        rows.append(jnp.concatenate([block[at : at + N, :N].T, block[at : at + N, N:].T], 1))
    return jnp.concatenate(rows, 0)


def all_positions(rows, offs, z, probe, amp, fwd, bwd, left, right, loss):
    clear(left, right, loss)
    lane = lax.broadcasted_iota(jnp.int32, (N, N), 1)

    def group(g, carry):
        first = g * GROUP
        waves, places = [], []
        for u in range(GROUP):
            top, off = rows[first + u], offs[first + u]
            inside = lane >= off
            patch = [
                pltpu.roll(jnp.where(inside, z[0, k, pl.ds(top, N), :], z[1, k, pl.ds(top, N), :]), (N - off) & (N - 1), 1)
                for k in range(2)
            ]
            for m in range(2):
                re, im = probe[m, 0], probe[m, 1]
                waves.append(jnp.concatenate([re * patch[0] - im * patch[1], re * patch[1] + im * patch[0]], 1))
            places.append((top, off, inside))
        wave = times_table(flip_blocks(times_table(jnp.concatenate(waves, 0), fwd[...])), fwd[...])
        backs = []
        total = jnp.zeros((8, N), f32)
        for u in range(GROUP):
            w = wave[u * 2 * N : (u + 1) * 2 * N]
            square = w * w
            square = square[:N] + square[N:]
            square = square[:, :N] + square[:, N:] + STABILIZER
            inverse = lax.rsqrt(square)
            measured = amp[first + u].T
            miss = square * inverse - measured
            total = total + jnp.sum((miss * miss).reshape(N // 8, 8, N), 0)
            weight = 1.0 - measured * inverse
            weight = jnp.concatenate([weight, weight], 1)
            backs += [weight * w[:N], weight * w[N:]]
        loss[...] += total
        back = times_table(flip_blocks(times_table(jnp.concatenate(backs, 0), bwd[...])), bwd[...])
        for u, (top, off, inside) in enumerate(places):
            grad_re, grad_im = 0.0, 0.0
            for m in range(2):
                re, im = probe[m, 0], probe[m, 1]
                b = back[(2 * u + m) * N : (2 * u + m + 1) * N]
                grad_re = grad_re + re * b[:, :N] + im * b[:, N:]
                grad_im = grad_im + re * b[:, N:] - im * b[:, :N]
            for k, grad in ((0, grad_re), (1, grad_im)):
                moved = pltpu.roll(grad, off, 1)
                left[k, pl.ds(top, N), :] += jnp.where(inside, moved, 0.0)
                right[k, pl.ds(top, N), :] += jnp.where(inside, 0.0, moved)
        return carry

    lax.fori_loop(0, 16 // GROUP, group, 0)


def clear(*refs):
    for ref in refs:
        ref[...] = jnp.zeros_like(ref)


def unit(tile, k, u):
    return tile[k, :, u * N : (u + 1) * N]


def chunk_of(ref, d):
    return ref.at[d // 8, pl.ds(32 * (d % 8), 32)]


def even_first(rows, offs, beta, z0, obj, probe, amp, fwd, bwd, even_low, even_high, ahead, loss):
    all_positions(rows, offs, z0, probe, amp, fwd, bwd, even_low, even_high, loss)
    b = beta[1]
    for k in range(2):
        ahead[k] = (1.0 + b) * (z0[0, k] - STEP * even_low[k]) - b * unit(obj, k, 0)


def odd_first(rows, offs, z0, halo, probe, amp, fwd, bwd, odd_low, odd_high, loss, z):
    z[0] = z0[1]
    for d in range(16):
        chunk_of(z.at[1], d)[...] = halo[d]
    all_positions(rows, offs, z, probe, amp, fwd, bwd, odd_low, odd_high, loss)


def odd_second(
    rows, offs, beta, z0, obj, even_high, odd_low, odd_high, ahead, probe, amp, fwd, bwd,
    mid, low_second, high_second, loss, z,
):
    b = beta[1]
    scale = (1.0 + b) * STEP
    for k in range(2):
        now = z0[1, k] - STEP * (even_high[k] + odd_low[k])
        mid[k] = now + b * (now - unit(obj, k, 1))
        z[0, k] = mid[k]
    for d in range(16):
        chunk_of(z.at[1], d)[...] = ahead[d, :32] - scale * chunk_of(odd_high, d)[...]
    all_positions(rows, offs, z, probe, amp, fwd, bwd, low_second, high_second, loss)


def even_second(
    rows, offs, beta, ahead, from_left, mid, odd_low, loss_a, loss_b, loss_c, probe, amp, fwd, bwd,
    tile, sums, even_low, even_high, loss, z,
):
    scale = (1.0 + beta[1]) * STEP
    for d in range(16):
        chunk_of(z.at[0], d)[...] = chunk_of(ahead, d)[...] - scale * from_left[d]
    z[1] = mid[...]
    all_positions(rows, offs, z, probe, amp, fwd, bwd, even_low, even_high, loss)
    for k in range(2):
        tile[k, :, :N] = z[0, k] - STEP * even_low[k]
        tile[k, :, N:] = z[1, k] - STEP * (even_high[k] + odd_low[k])
    before = jnp.sum(loss_a[...] + loss_b[...], axis=0, keepdims=True)
    after = jnp.sum(loss_c[...] + loss[...], axis=0, keepdims=True)
    lane = lax.broadcasted_iota(jnp.int32, (1, N), 1)
    line = jnp.where(lane < N // 2, before + pltpu.roll(before, N // 2, 1), after + pltpu.roll(after, N // 2, 1))
    sums[...] = jnp.broadcast_to(line, sums.shape)


def run(kernel, steps, args, outs, scratch, flops):
    whole = lambda a: pl.BlockSpec(a.shape, lambda i, n=len(a.shape): (0,) * n)
    out_shape = [jax.ShapeDtypeStruct(s, d) for s, d, _ in outs]
    return pl.pallas_call(
        kernel,
        grid=(steps,),
        out_shape=out_shape,
        in_specs=[spec or whole(a) for a, spec in args],
        out_specs=[spec or whole(o) for o, (_, _, spec) in zip(out_shape, outs)],
        scratch_shapes=scratch,
        compiler_params=pltpu.CompilerParams(vmem_limit_bytes=VMEM_BYTES),
        cost_estimate=pl.CostEstimate(flops=flops, bytes_accessed=2**22, transcendentals=0),
    )(*[a for a, _ in args])


def small_call(kernel, args, outs, scratch=()):
    return pl.pallas_call(
        kernel,
        out_shape=[jax.ShapeDtypeStruct(s, d) for s, d, _ in outs],
        in_specs=[spec for _, spec in args],
        out_specs=[spec for _, _, spec in outs],
        scratch_shapes=list(scratch),
        compiler_params=pltpu.CompilerParams(vmem_limit_bytes=VMEM_BYTES),
    )(*[a for a, _ in args])


def start_all(pairs, sems):
    copies = [pltpu.make_async_copy(a, b, sems.at[i]) for i, (a, b) in enumerate(pairs)]
    for c in copies:
        c.start()
    return copies


def prepare(
    owner_map, row_tops, restart, table, cols, obj, prev, amp,
    z0, send, rows, inv, right, left, beta, sems,
):
    band = lax.axis_index("ty")
    for c in range(16):
        owner = owner_map[band, c]
        inv[owner] = c
        right[owner] = owner_map[band, (c + 1) % 16]
        left[owner] = owner_map[band, (c + 15) % 16]
        rows[c] = row_tops[band * 16 + c]
    copies = start_all([(amp.at[2 * inv[d]], send.at[d, pl.ds(0, N)]) for d in range(16)], sems)
    for k in range(2):
        beta[k] = (table[restart[k] - 1] - 1.0) / table[restart[k]]
    b = beta[0]
    for u in range(2):
        for k in range(2):
            now = unit(obj, k, u)
            z0[u, k] = now + b * (now - unit(prev, k, u))
    lane = lax.broadcasted_iota(jnp.int32, (8, N), 1)
    for d in range(16):
        col = inv[d]
        even = cols[0, 2 * col] - 2 * N * col
        odd = cols[0, 2 * col + 1] - 2 * N * col - N
        send[d, N : N + 32] = chunk_of(z0.at[0], d)[...]
        send[d, N + 32 :] = jnp.where(lane < N // 2, even, odd).astype(f32)
    for c in copies:
        c.wait()


def pass_halo(right, inv, got, amp, send, off_even, off_odd, places, sems, more_sems):
    copies = start_all([(got.at[:, pl.ds(N + 32, 8)], places)], more_sems.at[pl.ds(16, 1)])
    copies += start_all([(amp.at[2 * inv[d] + 1], send.at[d, pl.ds(0, N)]) for d in range(16)], sems)
    copies += start_all([(got.at[right[d], pl.ds(N, 32)], send.at[d, pl.ds(N, 32)]) for d in range(16)], more_sems)
    copies[0].wait()
    for r in range(16):
        off_even[r] = places[r, 0, 0].astype(jnp.int32)
        off_odd[r] = places[r, 0, N // 2].astype(jnp.int32)
    for c in copies[1:]:
        c.wait()


def pass_ahead(right, ahead, odd_high, send):
    for d in range(16):
        send[d, :32] = ahead[right[d]]
        send[d, 32:] = chunk_of(odd_high, d)[...]


def pass_left(left, got, send):
    for d in range(16):
        send[d] = got[left[d], 32:]


def pass_last(left, got, sums, send):
    for d in range(16):
        send[d, :32] = got[left[d]]
        send[d, 32:] = sums[...]


def finish(tile, got, out, sums):
    total = got[0, 32:]
    for d in range(1, 16):
        total = total + got[d, 32:]
    sums[...] = total
    for k in range(2):
        out[k, :, N:] = tile[k, :, N:]
    for d in range(16):
        at = pl.ds(32 * (d % 8), 32)
        out[d // 8, at, :N] = tile[d // 8, at, :N] - STEP * got[d, :32]


def swap(block, axis="tx"):
    return lax.all_to_all(block, axis, 0, 0, tiled=True)


def shards(obj, prev, probe, amplitude, row_tops, scan_cols, restart, owner_map):
    fwd, bwd = dft_tables()
    ints = ((16,), jnp.int32, SMEM)
    unit_out, loss_out = ((2, 256, N), f32, None), ((8, N), f32, None)
    z_vmem = pltpu.VMEM((2, 2, 256, N), f32)
    unit_vmem = pltpu.VMEM((2, 256, N), f32)
    images = pl.BlockSpec((16, N, N), lambda i: (0, 0, 0))
    edge = pl.BlockSpec((16, 32, N), lambda i: (0, N // 32, 0))
    plain = lambda *arrays: [(a, None) for a in arrays]
    small = lambda *arrays: [(a, SMEM) for a in arrays]
    flops = 16 * 400_000_000

    z0, send, rows, inv, right, left, beta = small_call(
        prepare,
        small(owner_map, row_tops, restart, momentum_table(), scan_cols) + [(obj, VMEM), (prev, VMEM), (amplitude[0], ANY)],
        [((2, 2, 256, N), f32, VMEM), ((16, N + 40, N), f32, VMEM), ints, ints, ints, ints, ((2,), f32, SMEM)],
        [pltpu.SemaphoreType.DMA((16,))],
    )
    amp_even = swap(send)
    send, off_even, off_odd = small_call(
        pass_halo,
        small(right, inv) + [(amp_even, ANY), (amplitude[0], ANY)],
        [((16, N + 32, N), f32, VMEM), ints, ints],
        [pltpu.SMEM((16, 8, N), f32), pltpu.SemaphoreType.DMA((16,)), pltpu.SemaphoreType.DMA((17,))],
    )
    amp_odd = swap(send)
    even_low, even_high, ahead, loss_a = run(
        even_first, 1, small(rows, off_even, beta) + plain(z0, obj, probe) + [(amp_even, images)] + plain(fwd, bwd),
        [unit_out, unit_out, unit_out, loss_out], [], flops,
    )
    got = swap(ahead.reshape(16, 32, N))
    odd_low, odd_high, loss_b = run(
        odd_first, 1,
        small(rows, off_odd) + plain(z0) + [(amp_odd, edge)] + plain(probe) + [(amp_odd, images)] + plain(fwd, bwd),
        [unit_out, unit_out, loss_out], [z_vmem], flops,
    )
    (send,) = small_call(
        pass_ahead, small(right) + [(got, VMEM), (odd_high, VMEM)], [((16, 64, N), f32, VMEM)]
    )
    got = swap(send)
    (send,) = small_call(pass_left, small(left) + [(got, VMEM)], [((16, 32, N), f32, VMEM)])
    from_left = swap(send)
    mid, odd_low_second, odd_high_second, loss_c = run(
        odd_second, 1,
        small(rows, off_odd, beta) + plain(z0, obj, even_high, odd_low, odd_high, got, probe)
        + [(amp_odd, images)] + plain(fwd, bwd),
        [unit_out, unit_out, unit_out, loss_out], [z_vmem], flops,
    )
    last = swap(odd_high_second.reshape(16, 32, N))
    tile, sums = run(
        even_second, 1,
        small(rows, off_even, beta) + plain(ahead, from_left, mid, odd_low_second, loss_a, loss_b, loss_c, probe)
        + [(amp_even, images)] + plain(fwd, bwd),
        [((2, 256, 256), f32, None), loss_out], [unit_vmem, unit_vmem, pltpu.VMEM((8, N), f32), z_vmem], flops,
    )
    (send,) = small_call(
        pass_last, small(left) + [(last, VMEM), (sums, VMEM)], [((16, 40, N), f32, VMEM)]
    )
    got = swap(send)
    tile, sums = small_call(
        finish, [(tile, VMEM), (got, VMEM)], [((2, 256, 256), f32, VMEM), ((8, N), f32, VMEM)]
    )
    sums = swap(sums, "ty")
    losses = jnp.sum(jnp.sum(sums, axis=0).reshape(2, N // 2), axis=1) * (0.5 / 67108864.0)
    return (tile, losses)


def solution(mesh):
    in_specs = (
        P(None, "ty", "tx"),
        P(None, "ty", "tx"),
        P(),
        P(("ty", "tx"), None, None, None),
        P(),
        P(("ty", "tx"), None),
        P(),
        P(),
    )
    return jax.shard_map(
        shards, mesh=mesh, in_specs=in_specs, out_specs=(P(None, "ty", "tx"), P()), check_vma=False
    )
```

```python
import functools
import math

import jax
import jax.numpy as jnp
import ml_dtypes
import numpy as np
from jax import lax
from jax.experimental import pallas as pl
from jax.experimental.pallas import tpu as pltpu
from jax.sharding import PartitionSpec as P

START = 100
STABILIZER = 0.05
STEP = 0.25
N = 128
GROUP = 8
VMEM_BYTES = 60 * 2**20
f32 = jnp.float32
bf16 = jnp.bfloat16
SMEM = pl.BlockSpec(memory_space=pltpu.SMEM)
VMEM = pl.BlockSpec(memory_space=pltpu.VMEM)
ANY = pl.BlockSpec(memory_space=pl.ANY)


def momentum_table():
    values = [1.0]
    for counter in range(START):
        last = values[-1]
        values.append((1.0 + (1.0 + 4.0 * last * last) ** 0.5) / 2.0)
    return jnp.asarray(values, f32)


def dft_tables():
    index = np.arange(N)
    angle = (index[:, None] * index[None, :] % N).astype(np.float64) * (2.0 * math.pi / N)
    cos, sin = np.cos(angle) / math.sqrt(N), np.sin(angle) / math.sqrt(N)

    def stacked(table):
        high = table.astype(ml_dtypes.bfloat16)
        low = (table - high.astype(np.float64)).astype(ml_dtypes.bfloat16)
        return jnp.asarray(np.concatenate([high, high, low], 0))

    return stacked(np.block([[cos, -sin], [sin, cos]])), stacked(np.block([[cos, sin], [-sin, cos]]))


def times_table(block, table):
    parts = []
    for at in range(0, GROUP * 2 * N, N):
        if isinstance(block, tuple):
            high, low = block[0][at : at + N], block[1][at : at + N]
        else:
            part = block[at : at + N]
            high = part.astype(bf16)
            low = (part - high.astype(f32)).astype(bf16)
        parts.append(jnp.dot(jnp.concatenate([high, low, high], 1), table, preferred_element_type=f32))
    return jnp.concatenate(parts, 0)


def flip_blocks(block):
    rows = []
    for at in range(0, block.shape[0], N):
        rows.append(jnp.concatenate([block[at : at + N, :N].T, block[at : at + N, N:].T], 1))
    return jnp.concatenate(rows, 0)


def way_out(rows, offs, z, probe, amp, amp_first, fwd, loss, first):
    lane = lax.broadcasted_iota(jnp.int32, (N, N), 1)
    waves = []
    for u in range(GROUP):
        top, off = rows[first + u], offs[first + u]
        inside = lane >= off
        patch = [
            pltpu.roll(jnp.where(inside, z[0, k, pl.ds(top, N), :], z[1, k, pl.ds(top, N), :]), (N - off) & (N - 1), 1)
            for k in range(2)
        ]
        for m in range(2):
            re, im = probe[m, 0], probe[m, 1]
            waves.append(jnp.concatenate([re * patch[0] - im * patch[1], re * patch[1] + im * patch[0]], 1))
    wave = times_table(flip_blocks(times_table(jnp.concatenate(waves, 0), fwd[...])), fwd[...])
    weighted = []
    total = jnp.zeros((8, N), f32)
    for u in range(GROUP):
        w = wave[u * 2 * N : (u + 1) * 2 * N]
        square = w * w
        square = square[:N] + square[N:]
        square = square[:, :N] + square[:, N:] + STABILIZER
        inverse = lax.rsqrt(square)
        measured = amp[amp_first + u].T
        miss = square * inverse - measured
        total = total + jnp.sum((miss * miss).reshape(N // 8, 8, N), 0)
        weight = 1.0 - measured * inverse
        weight = jnp.concatenate([weight, weight], 1)
        weighted += [weight * w[:N], weight * w[N:]]
    loss[...] += total
    return jnp.concatenate(weighted, 0)


def way_back(rows, offs, probe, weighted, bwd, left, right, first):
    lane = lax.broadcasted_iota(jnp.int32, (N, N), 1)
    back = times_table(flip_blocks(times_table(weighted, bwd[...])), bwd[...])
    for u in range(GROUP):
        top, off = rows[first + u], offs[first + u]
        inside = lane >= off
        grad_re, grad_im = 0.0, 0.0
        for m in range(2):
            re, im = probe[m, 0], probe[m, 1]
            b = back[(2 * u + m) * N : (2 * u + m + 1) * N]
            grad_re = grad_re + re * b[:, :N] + im * b[:, N:]
            grad_im = grad_im + re * b[:, N:] - im * b[:, :N]
        for k, grad in ((0, grad_re), (1, grad_im)):
            moved = pltpu.roll(grad, off, 1)
            left[k, pl.ds(top, N), :] += jnp.where(inside, moved, 0.0)
            right[k, pl.ds(top, N), :] += jnp.where(inside, 0.0, moved)


def all_positions(rows, offs, z, probe, amp, fwd, bwd, left, right, loss):
    clear(left, right, loss)

    def group(g, carry):
        first = g * GROUP
        weighted = way_out(rows, offs, z, probe, amp, first, fwd, loss, first)
        way_back(rows, offs, probe, weighted, bwd, left, right, first)
        return carry

    lax.fori_loop(0, 16 // GROUP, group, 0)


def clear(*refs):
    for ref in refs:
        ref[...] = jnp.zeros_like(ref)


def unit(tile, k, u):
    return tile[k, :, u * N : (u + 1) * N]


def chunk_of(ref, d):
    return ref.at[d // 8, pl.ds(32 * (d % 8), 32)]


def even_first(rows, offs, beta, obj, prev, probe, amp, fwd, bwd, z0, even_low, even_high, ahead, loss):
    for u in range(2):
        for k in range(2):
            now = unit(obj, k, u)
            z0[u, k] = now + beta[0] * (now - unit(prev, k, u))
    all_positions(rows, offs, z0, probe, amp, fwd, bwd, even_low, even_high, loss)
    b = beta[1]
    for k in range(2):
        ahead[k] = (1.0 + b) * (z0[0, k] - STEP * even_low[k]) - b * unit(obj, k, 0)


def odd_first(rows, offs, z0, halo, probe, amp, fwd, bwd, odd_low, odd_high, loss, z):
    z[0] = z0[1]
    for d in range(16):
        chunk_of(z.at[1], d)[...] = halo[d]
    all_positions(rows, offs, z, probe, amp, fwd, bwd, odd_low, odd_high, loss)


def odd_second(
    rows, offs, beta, z0, obj, even_high, odd_low, odd_high, ahead, probe, amp, fwd, bwd,
    mid, low_second, high_second, loss, z,
):
    b = beta[1]
    scale = (1.0 + b) * STEP
    for k in range(2):
        now = z0[1, k] - STEP * (even_high[k] + odd_low[k])
        mid[k] = now + b * (now - unit(obj, k, 1))
        z[0, k] = mid[k]
    for d in range(16):
        chunk_of(z.at[1], d)[...] = ahead[d, :32] - scale * chunk_of(odd_high, d)[...]
    all_positions(rows, offs, z, probe, amp, fwd, bwd, low_second, high_second, loss)


def even_out(rows, offs, beta, ahead, from_left, mid, loss_a, loss_b, loss_c, probe, amp, fwd, start, sums, high, low, loss, z):
    @pl.when(pl.program_id(0) == 0)
    def _():
        clear(loss)
        scale = (1.0 + beta[1]) * STEP
        for d in range(16):
            chunk_of(z.at[0], d)[...] = chunk_of(ahead, d)[...] - scale * from_left[d]
        z[1] = mid[...]
        start[...] = z[0]

    weighted = way_out(rows, offs, z, probe, amp, 0, fwd, loss, pl.program_id(0) * GROUP)
    high[...] = weighted.astype(bf16)
    low[...] = (weighted - high[...].astype(f32)).astype(bf16)

    @pl.when(pl.program_id(0) == pl.num_programs(0) - 1)
    def _():
        before = jnp.sum(loss_a[...] + loss_b[...], axis=0, keepdims=True)
        after = jnp.sum(loss_c[...] + loss[...], axis=0, keepdims=True)
        lane = lax.broadcasted_iota(jnp.int32, (1, N), 1)
        line = jnp.where(lane < N // 2, before + pltpu.roll(before, N // 2, 1), after + pltpu.roll(after, N // 2, 1))
        sums[...] = jnp.broadcast_to(line, sums.shape)


def even_back(rows, offs, start, mid, odd_low, probe, high, low, bwd, tile, done, even_low, even_high):
    @pl.when(pl.program_id(0) == 0)
    def _():
        clear(even_low, even_high, done)

    way_back(rows, offs, probe, (high, low), bwd, even_low, even_high, pl.program_id(0) * GROUP)

    @pl.when(pl.program_id(0) == pl.num_programs(0) - 1)
    def _():
        for k in range(2):
            tile[k, :, :N] = start[k] - STEP * even_low[k]
            tile[k, :, N:] = mid[k] - STEP * (even_high[k] + odd_low[k])


def run(kernel, steps, args, outs, scratch, flops, limit=VMEM_BYTES):
    whole = lambda a: pl.BlockSpec(a.shape, lambda i, n=len(a.shape): (0,) * n)
    out_shape = [jax.ShapeDtypeStruct(s, d) for s, d, _ in outs]
    return pl.pallas_call(
        kernel,
        grid=(steps,),
        out_shape=out_shape,
        in_specs=[spec or whole(a) for a, spec in args],
        out_specs=[spec or whole(o) for o, (_, _, spec) in zip(out_shape, outs)],
        scratch_shapes=scratch,
        compiler_params=pltpu.CompilerParams(vmem_limit_bytes=limit),
        cost_estimate=pl.CostEstimate(flops=flops, bytes_accessed=2**22, transcendentals=0),
    )(*[a for a, _ in args])


def small_call(kernel, args, outs, scratch=(), limit=6 * 2**20):
    return pl.pallas_call(
        kernel,
        out_shape=[jax.ShapeDtypeStruct(s, d) for s, d, _ in outs],
        in_specs=[spec for _, spec in args],
        out_specs=[spec for _, _, spec in outs],
        scratch_shapes=list(scratch),
        compiler_params=pltpu.CompilerParams(vmem_limit_bytes=limit),
    )(*[a for a, _ in args])


def start_all(pairs, sems):
    copies = [pltpu.make_async_copy(a, b, sems.at[i]) for i, (a, b) in enumerate(pairs)]
    for c in copies:
        c.start()
    return copies


def prepare(
    owner_map, row_tops, restart, table, cols, obj, prev, amp, send, rows, inv, right, left, beta, now, before, sems
):
    edges = start_all([(obj.at[:, :, pl.ds(0, N)], now), (prev.at[:, :, pl.ds(0, N)], before)], sems.at[pl.ds(16, 2)])
    band = lax.axis_index("ty")
    for c in range(16):
        owner = owner_map[band, c]
        inv[owner] = c
        right[owner] = owner_map[band, (c + 1) % 16]
        left[owner] = owner_map[band, (c + 15) % 16]
        rows[c] = row_tops[band * 16 + c]
    copies = start_all([(amp.at[2 * inv[d]], send.at[d, pl.ds(0, N)]) for d in range(16)], sems)
    for k in range(2):
        beta[k] = (table[restart[k] - 1] - 1.0) / table[restart[k]]
    for c in edges:
        c.wait()
    now[...] = now[...] + beta[0] * (now[...] - before[...])
    lane = lax.broadcasted_iota(jnp.int32, (8, N), 1)
    for d in range(16):
        col = inv[d]
        even = cols[0, 2 * col] - 2 * N * col
        odd = cols[0, 2 * col + 1] - 2 * N * col - N
        send[d, N : N + 32] = chunk_of(now, d)[...]
        send[d, N + 32 :] = jnp.where(lane < N // 2, even, odd).astype(f32)
    for c in copies:
        c.wait()


def pass_halo(right, inv, got, amp, send, off_even, off_odd, places, sems):
    fetch_places = pltpu.make_async_copy(got.at[:, pl.ds(N + 32, 1)], places, sems.at[32])
    fetch_places.start()
    copies = start_all(
        [(amp.at[2 * inv[d] + 1], send.at[d, pl.ds(0, N)]) for d in range(16)]
        + [(got.at[right[d], pl.ds(N, 32)], send.at[d, pl.ds(N, 32)]) for d in range(16)],
        sems,
    )
    fetch_places.wait()
    for r in range(16):
        off_even[r] = places[r, 0, 0].astype(jnp.int32)
        off_odd[r] = places[r, 0, N // 2].astype(jnp.int32)
    for c in copies:
        c.wait()


def pass_ahead(right, ahead, odd_high, send):
    for d in range(16):
        send[d, :32] = ahead[right[d]]
        send[d, 32:] = chunk_of(odd_high, d)[...]


def pass_left(left, got, send):
    for d in range(16):
        send[d] = got[left[d], 32:]


def pass_last(left, got, sums, send):
    for d in range(16):
        send[d, :32] = got[left[d]]
        send[d, 32:] = sums[...]


def finish(tile, got, out):
    for d in range(16):
        at = pl.ds(32 * (d % 8), 32)
        out[d // 8, at] = tile[d // 8, at] - STEP * got[d]


def swap(block, axis="tx"):
    return lax.all_to_all(block, axis, 0, 0, tiled=True)


def shards(obj, prev, probe, amplitude, row_tops, scan_cols, restart, owner_map):
    fwd, bwd = dft_tables()
    ints = ((16,), jnp.int32, SMEM)
    unit_out, loss_out = ((2, 256, N), f32, None), ((8, N), f32, None)
    z_vmem = pltpu.VMEM((2, 2, 256, N), f32)
    unit_vmem = pltpu.VMEM((2, 256, N), f32)
    images = pl.BlockSpec((16, N, N), lambda i: (0, 0, 0))
    edge = pl.BlockSpec((16, 32, N), lambda i: (0, N // 32, 0))
    plain = lambda *arrays: [(a, None) for a in arrays]
    small = lambda *arrays: [(a, SMEM) for a in arrays]
    flops = 16 * 400_000_000

    amplitude = amplitude[0]
    send, rows, inv, right, left, beta = small_call(
        prepare,
        small(owner_map, row_tops, restart, momentum_table(), scan_cols)
        + [(obj, ANY), (prev, ANY), (amplitude, ANY)],
        [((16, N + 40, N), f32, VMEM), ints, ints, ints, ints, ((2,), f32, SMEM)],
        [unit_vmem, unit_vmem, pltpu.SemaphoreType.DMA((18,))], limit=VMEM_BYTES,
    )
    amp_even = swap(send)
    send, off_even, off_odd = small_call(
        pass_halo, small(right, inv) + [(amp_even, ANY), (amplitude, ANY)],
        [((16, N + 32, N), f32, VMEM), ints, ints],
        [pltpu.SMEM((16, 1, N), f32), pltpu.SemaphoreType.DMA((33,))], limit=VMEM_BYTES,
    )
    amp_odd = swap(send)
    z0, even_low, even_high, ahead, loss_a = run(
        even_first, 1, small(rows, off_even, beta) + plain(obj, prev, probe) + [(amp_even, images)] + plain(fwd, bwd),
        [((2, 2, 256, N), f32, None), unit_out, unit_out, unit_out, loss_out], [], flops,
    )
    got = swap(ahead.reshape(16, 32, N))
    odd_low, odd_high, loss_b = run(
        odd_first, 1,
        small(rows, off_odd) + plain(z0) + [(amp_odd, edge)] + plain(probe) + [(amp_odd, images)] + plain(fwd, bwd),
        [unit_out, unit_out, loss_out], [z_vmem], flops,
    )
    (send,) = small_call(
        pass_ahead, small(right) + [(got, VMEM), (odd_high, VMEM)], [((16, 64, N), f32, VMEM)]
    )
    got = swap(send)
    (send,) = small_call(pass_left, small(left) + [(got, VMEM)], [((16, 32, N), f32, VMEM)])
    from_left = swap(send)
    mid, odd_low_second, odd_high_second, loss_c = run(
        odd_second, 1,
        small(rows, off_odd, beta) + plain(z0, obj, even_high, odd_low, odd_high, got, probe)
        + [(amp_odd, images)] + plain(fwd, bwd),
        [unit_out, unit_out, unit_out, loss_out], [z_vmem], flops,
    )
    last = swap(odd_high_second.reshape(16, 32, N))
    half_block = pl.BlockSpec((GROUP * 2 * N, 2 * N), lambda i: (i, 0))
    half_out = ((16 * 2 * N, 2 * N), bf16, half_block)
    start, sums, high, low = run(
        even_out, 16 // GROUP,
        small(rows, off_even, beta) + plain(ahead, from_left, mid, loss_a, loss_b, loss_c, probe)
        + [(amp_even, pl.BlockSpec((GROUP, N, N), lambda i: (i, 0, 0)))] + plain(fwd),
        [unit_out, loss_out, half_out, half_out], [pltpu.VMEM((8, N), f32), z_vmem], flops // 2,
    )
    (send,) = small_call(
        pass_last, small(left) + [(last, VMEM), (sums, VMEM)], [((16, 40, N), f32, VMEM)]
    )
    got = swap(send)
    tile, done = run(
        even_back, 16 // GROUP,
        small(rows, off_even) + plain(start, mid, odd_low_second, probe)
        + [(high, half_block), (low, half_block)] + plain(bwd),
        [((2, 256, 256), f32, None), loss_out], [unit_vmem, unit_vmem], flops // 2,
    )
    sums = jnp.sum(got[:, 32:], axis=0) + done
    sums = swap(sums, "ty")
    left_block = pl.BlockSpec((2, 256, N), lambda i: (0, 0, 0))
    tile = pl.pallas_call(
        finish,
        grid=(1,),
        out_shape=jax.ShapeDtypeStruct((2, 256, 256), f32),
        in_specs=[left_block, pl.BlockSpec((16, 32, N), lambda i: (0, 0, 0))],
        out_specs=left_block,
        input_output_aliases={0: 0},
        compiler_params=pltpu.CompilerParams(vmem_limit_bytes=VMEM_BYTES),
    )(tile, got)
    losses = jnp.sum(jnp.sum(sums, axis=0).reshape(2, N // 2), axis=1) * (0.5 / 67108864.0)
    return (tile, losses)


def solution(mesh):
    in_specs = (
        P(None, "ty", "tx"),
        P(None, "ty", "tx"),
        P(),
        P(("ty", "tx"), None, None, None),
        P(),
        P(("ty", "tx"), None),
        P(),
        P(),
    )
    return jax.shard_map(
        shards, mesh=mesh, in_specs=in_specs, out_specs=(P(None, "ty", "tx"), P()), check_vma=False
    )
```

```python
import functools
import math

import jax
import jax.numpy as jnp
import ml_dtypes
import numpy as np
from jax import lax
from jax.experimental import pallas as pl
from jax.experimental.pallas import tpu as pltpu
from jax.sharding import PartitionSpec as P

START = 100
STABILIZER = 0.05
STEP = 0.25
N = 128
GROUP = 8
VMEM_BYTES = 60 * 2**20
f32 = jnp.float32
bf16 = jnp.bfloat16
SMEM = pl.BlockSpec(memory_space=pltpu.SMEM)
VMEM = pl.BlockSpec(memory_space=pltpu.VMEM)
ANY = pl.BlockSpec(memory_space=pl.ANY)


def momentum_table():
    values = [1.0]
    for counter in range(START):
        last = values[-1]
        values.append((1.0 + (1.0 + 4.0 * last * last) ** 0.5) / 2.0)
    return jnp.asarray(values, f32)


def dft_tables():
    index = np.arange(N)
    angle = (index[:, None] * index[None, :] % N).astype(np.float64) * (2.0 * math.pi / N)
    cos, sin = np.cos(angle) / math.sqrt(N), np.sin(angle) / math.sqrt(N)

    def stacked(table):
        high = table.astype(ml_dtypes.bfloat16)
        low = (table - high.astype(np.float64)).astype(ml_dtypes.bfloat16)
        return jnp.asarray(np.concatenate([high, high, low], 0))

    return stacked(np.block([[cos, -sin], [sin, cos]])), stacked(np.block([[cos, sin], [-sin, cos]]))


def times_table(block, table):
    parts = []
    for at in range(0, GROUP * 2 * N, N):
        if isinstance(block, tuple):
            high, low = block[0][at : at + N], block[1][at : at + N]
        else:
            part = block[at : at + N]
            high = part.astype(bf16)
            low = (part - high.astype(f32)).astype(bf16)
        parts.append(jnp.dot(jnp.concatenate([high, low, high], 1), table, preferred_element_type=f32))
    return jnp.concatenate(parts, 0)


def flip_blocks(block):
    rows = []
    for at in range(0, block.shape[0], N):
        rows.append(jnp.concatenate([block[at : at + N, :N].T, block[at : at + N, N:].T], 1))
    return jnp.concatenate(rows, 0)


def way_out(rows, offs, z, probe, amp, amp_first, fwd, loss, first):
    lane = lax.broadcasted_iota(jnp.int32, (N, N), 1)
    waves = []
    for u in range(GROUP):
        top, off = rows[first + u], offs[first + u]
        inside = lane >= off
        patch = [
            pltpu.roll(jnp.where(inside, z[0, k, pl.ds(top, N), :], z[1, k, pl.ds(top, N), :]), (N - off) & (N - 1), 1)
            for k in range(2)
        ]
        for m in range(2):
            re, im = probe[m, 0], probe[m, 1]
            waves.append(jnp.concatenate([re * patch[0] - im * patch[1], re * patch[1] + im * patch[0]], 1))
    wave = times_table(flip_blocks(times_table(jnp.concatenate(waves, 0), fwd[...])), fwd[...])
    weighted = []
    total = jnp.zeros((8, N), f32)
    for u in range(GROUP):
        w = wave[u * 2 * N : (u + 1) * 2 * N]
        square = w * w
        square = square[:N] + square[N:]
        square = square[:, :N] + square[:, N:] + STABILIZER
        inverse = lax.rsqrt(square)
        measured = amp[amp_first + u].T
        miss = square * inverse - measured
        total = total + jnp.sum((miss * miss).reshape(N // 8, 8, N), 0)
        weight = 1.0 - measured * inverse
        weight = jnp.concatenate([weight, weight], 1)
        weighted += [weight * w[:N], weight * w[N:]]
    loss[...] += total
    return jnp.concatenate(weighted, 0)


def way_back(rows, offs, probe, weighted, bwd, left, right, first):
    lane = lax.broadcasted_iota(jnp.int32, (N, N), 1)
    back = times_table(flip_blocks(times_table(weighted, bwd[...])), bwd[...])
    for u in range(GROUP):
        top, off = rows[first + u], offs[first + u]
        inside = lane >= off
        grad_re, grad_im = 0.0, 0.0
        for m in range(2):
            re, im = probe[m, 0], probe[m, 1]
            b = back[(2 * u + m) * N : (2 * u + m + 1) * N]
            grad_re = grad_re + re * b[:, :N] + im * b[:, N:]
            grad_im = grad_im + re * b[:, N:] - im * b[:, :N]
        for k, grad in ((0, grad_re), (1, grad_im)):
            moved = pltpu.roll(grad, off, 1)
            left[k, pl.ds(top, N), :] += jnp.where(inside, moved, 0.0)
            right[k, pl.ds(top, N), :] += jnp.where(inside, 0.0, moved)


def all_positions(rows, offs, z, probe, amp, fwd, bwd, left, right, loss):
    clear(left, right, loss)

    def group(g, carry):
        first = g * GROUP
        weighted = way_out(rows, offs, z, probe, amp, first, fwd, loss, first)
        way_back(rows, offs, probe, weighted, bwd, left, right, first)
        return carry

    lax.fori_loop(0, 16 // GROUP, group, 0)


def clear(*refs):
    for ref in refs:
        ref[...] = jnp.zeros_like(ref)


def unit(tile, k, u):
    return tile[k, :, u * N : (u + 1) * N]


def chunk_of(ref, d):
    return ref.at[d // 8, pl.ds(32 * (d % 8), 32)]


def even_first(rows, offs, beta, obj, prev, probe, amp, fwd, bwd, z0, even_low, even_high, ahead, loss):
    for u in range(2):
        for k in range(2):
            now = unit(obj, k, u)
            z0[u, k] = now + beta[0] * (now - unit(prev, k, u))
    all_positions(rows, offs, z0, probe, amp, fwd, bwd, even_low, even_high, loss)
    b = beta[1]
    for k in range(2):
        ahead[k] = (1.0 + b) * (z0[0, k] - STEP * even_low[k]) - b * unit(obj, k, 0)


def odd_first(rows, offs, z0, halo, probe, amp, fwd, bwd, odd_low, odd_high, loss, z):
    z[0] = z0[0]
    for d in range(16):
        chunk_of(z.at[1], d)[...] = halo[d]
    all_positions(rows, offs, z, probe, amp, fwd, bwd, odd_low, odd_high, loss)


def odd_second(
    rows, offs, beta, z0, obj, even_high, odd_low, odd_high, ahead, probe, amp, fwd, bwd,
    mid, low_second, high_second, loss, z,
):
    b = beta[1]
    scale = (1.0 + b) * STEP
    for k in range(2):
        now = z0[0, k] - STEP * (even_high[k] + odd_low[k])
        mid[k] = now + b * (now - obj[k])
        z[0, k] = mid[k]
    for d in range(16):
        chunk_of(z.at[1], d)[...] = ahead[d, :32] - scale * chunk_of(odd_high, d)[...]
    all_positions(rows, offs, z, probe, amp, fwd, bwd, low_second, high_second, loss)


def even_out(rows, offs, beta, ahead, from_left, mid, loss_a, loss_b, loss_c, probe, amp, fwd, start, sums, high, low, loss, z):
    @pl.when(pl.program_id(0) == 0)
    def _():
        clear(loss)
        scale = (1.0 + beta[1]) * STEP
        for d in range(16):
            chunk_of(z.at[0], d)[...] = chunk_of(ahead, d)[...] - scale * from_left[d]
        z[1] = mid[...]
        start[...] = z[0]

    weighted = way_out(rows, offs, z, probe, amp, 0, fwd, loss, pl.program_id(0) * GROUP)
    high[...] = weighted.astype(bf16)
    low[...] = (weighted - high[...].astype(f32)).astype(bf16)

    @pl.when(pl.program_id(0) == pl.num_programs(0) - 1)
    def _():
        before = jnp.sum(loss_a[...] + loss_b[...], axis=0, keepdims=True)
        after = jnp.sum(loss_c[...] + loss[...], axis=0, keepdims=True)
        lane = lax.broadcasted_iota(jnp.int32, (1, N), 1)
        line = jnp.where(lane < N // 2, before + pltpu.roll(before, N // 2, 1), after + pltpu.roll(after, N // 2, 1))
        sums[...] = jnp.broadcast_to(line, sums.shape)


def even_back(rows, offs, start, mid, odd_low, probe, high, low, bwd, tile, even_low, even_high):
    @pl.when(pl.program_id(0) == 0)
    def _():
        clear(even_low, even_high)

    way_back(rows, offs, probe, (high, low), bwd, even_low, even_high, pl.program_id(0) * GROUP)

    @pl.when(pl.program_id(0) == pl.num_programs(0) - 1)
    def _():
        for k in range(2):
            tile[k, :, :N] = start[k] - STEP * even_low[k]
            tile[k, :, N:] = mid[k] - STEP * (even_high[k] + odd_low[k])


def run(kernel, steps, args, outs, scratch, flops, limit=VMEM_BYTES):
    whole = lambda a: pl.BlockSpec(a.shape, lambda i, n=len(a.shape): (0,) * n)
    out_shape = [jax.ShapeDtypeStruct(s, d) for s, d, _ in outs]
    return pl.pallas_call(
        kernel,
        grid=(steps,),
        out_shape=out_shape,
        in_specs=[spec or whole(a) for a, spec in args],
        out_specs=[spec or whole(o) for o, (_, _, spec) in zip(out_shape, outs)],
        scratch_shapes=scratch,
        compiler_params=pltpu.CompilerParams(vmem_limit_bytes=limit),
        cost_estimate=pl.CostEstimate(flops=flops, bytes_accessed=2**22, transcendentals=0),
    )(*[a for a, _ in args])


def small_call(kernel, args, outs, scratch=(), limit=6 * 2**20):
    return pl.pallas_call(
        kernel,
        out_shape=[jax.ShapeDtypeStruct(s, d) for s, d, _ in outs],
        in_specs=[spec for _, spec in args],
        out_specs=[spec for _, _, spec in outs],
        scratch_shapes=list(scratch),
        compiler_params=pltpu.CompilerParams(vmem_limit_bytes=limit),
    )(*[a for a, _ in args])


def start_all(pairs, sems):
    copies = [pltpu.make_async_copy(a, b, sems.at[i]) for i, (a, b) in enumerate(pairs)]
    for c in copies:
        c.start()
    return copies


def prepare(
    owner_map, row_tops, restart, table, cols, obj, prev, amp, send, rows, inv, right, left, beta, now, before, sems
):
    edges = start_all([(obj.at[:, :, pl.ds(0, N)], now), (prev.at[:, :, pl.ds(0, N)], before)], sems.at[pl.ds(16, 2)])
    band = lax.axis_index("ty")
    for c in range(16):
        owner = owner_map[band, c]
        inv[owner] = c
        right[owner] = owner_map[band, (c + 1) % 16]
        left[owner] = owner_map[band, (c + 15) % 16]
        rows[c] = row_tops[band * 16 + c]
    copies = start_all([(amp.at[2 * inv[d]], send.at[d, pl.ds(0, N)]) for d in range(16)], sems)
    for k in range(2):
        beta[k] = (table[restart[k] - 1] - 1.0) / table[restart[k]]
    for c in edges:
        c.wait()
    now[...] = now[...] + beta[0] * (now[...] - before[...])
    lane = lax.broadcasted_iota(jnp.int32, (8, N), 1)
    for d in range(16):
        col = inv[d]
        even = cols[0, 2 * col] - 2 * N * col
        odd = cols[0, 2 * col + 1] - 2 * N * col - N
        send[d, N : N + 32] = chunk_of(now, d)[...]
        send[d, N + 32 :] = jnp.where(lane < N // 2, even, odd).astype(f32)
    for c in copies:
        c.wait()


def pass_halo(right, inv, got, amp, send, off_even, off_odd, places, sems):
    fetch_places = pltpu.make_async_copy(got.at[:, pl.ds(N + 32, 1)], places, sems.at[32])
    fetch_places.start()
    copies = start_all(
        [(amp.at[2 * inv[d] + 1], send.at[d, pl.ds(0, N)]) for d in range(16)]
        + [(got.at[right[d], pl.ds(N, 32)], send.at[d, pl.ds(N, 32)]) for d in range(16)],
        sems,
    )
    fetch_places.wait()
    for r in range(16):
        off_even[r] = places[r, 0, 0].astype(jnp.int32)
        off_odd[r] = places[r, 0, N // 2].astype(jnp.int32)
    for c in copies:
        c.wait()


def pass_ahead(right, ahead, odd_high, send):
    for d in range(16):
        send[d, :32] = ahead[right[d]]
        send[d, 32:] = chunk_of(odd_high, d)[...]


def pass_left(left, got, send):
    for d in range(16):
        send[d] = got[left[d], 32:]


def pass_last(left, got, sums, send):
    for d in range(16):
        send[d, :32] = got[left[d]]
        send[d, 32:] = sums[...]


def finish(tile, got, out):
    for d in range(16):
        at = pl.ds(32 * (d % 8), 32)
        out[d // 8, at] = tile[d // 8, at] - STEP * got[d]


def swap(block, axis="tx"):
    return lax.all_to_all(block, axis, 0, 0, tiled=True)


def shards(obj, prev, probe, amplitude, row_tops, scan_cols, restart, owner_map):
    fwd, bwd = dft_tables()
    ints = ((16,), jnp.int32, SMEM)
    unit_out, loss_out = ((2, 256, N), f32, None), ((8, N), f32, None)
    z_vmem = pltpu.VMEM((2, 2, 256, N), f32)
    unit_vmem = pltpu.VMEM((2, 256, N), f32)
    images = pl.BlockSpec((16, N, N), lambda i: (0, 0, 0))
    right_unit = pl.BlockSpec((1, 2, 256, N), lambda i: (1, 0, 0, 0))
    edge = pl.BlockSpec((16, 32, N), lambda i: (0, N // 32, 0))
    plain = lambda *arrays: [(a, None) for a in arrays]
    small = lambda *arrays: [(a, SMEM) for a in arrays]
    flops = 16 * 400_000_000

    amplitude = amplitude[0]
    send, rows, inv, right, left, beta = small_call(
        prepare,
        small(owner_map, row_tops, restart, momentum_table(), scan_cols)
        + [(obj, ANY), (prev, ANY), (amplitude, ANY)],
        [((16, N + 40, N), f32, VMEM), ints, ints, ints, ints, ((2,), f32, SMEM)],
        [unit_vmem, unit_vmem, pltpu.SemaphoreType.DMA((18,))], limit=VMEM_BYTES,
    )
    amp_even = swap(send)
    send, off_even, off_odd = small_call(
        pass_halo, small(right, inv) + [(amp_even, ANY), (amplitude, ANY)],
        [((16, N + 32, N), f32, VMEM), ints, ints],
        [pltpu.SMEM((16, 1, N), f32), pltpu.SemaphoreType.DMA((33,))], limit=VMEM_BYTES,
    )
    amp_odd = swap(send)
    z0, even_low, even_high, ahead, loss_a = run(
        even_first, 1, small(rows, off_even, beta) + plain(obj, prev, probe) + [(amp_even, images)] + plain(fwd, bwd),
        [((2, 2, 256, N), f32, None), unit_out, unit_out, unit_out, loss_out], [], flops,
    )
    got = swap(ahead.reshape(16, 32, N))
    odd_low, odd_high, loss_b = run(
        odd_first, 1,
        small(rows, off_odd) + [(z0, right_unit), (amp_odd, edge)] + plain(probe) + [(amp_odd, images)] + plain(fwd, bwd),
        [unit_out, unit_out, loss_out], [z_vmem], flops,
    )
    (send,) = small_call(
        pass_ahead, small(right) + [(got, VMEM), (odd_high, VMEM)], [((16, 64, N), f32, VMEM)]
    )
    got = swap(send)
    (send,) = small_call(pass_left, small(left) + [(got, VMEM)], [((16, 32, N), f32, VMEM)])
    from_left = swap(send)
    mid, odd_low_second, odd_high_second, loss_c = run(
        odd_second, 1,
        small(rows, off_odd, beta) + [(z0, right_unit), (obj, pl.BlockSpec((2, 256, N), lambda i: (0, 0, 1)))]
        + plain(even_high, odd_low, odd_high, got, probe)
        + [(amp_odd, images)] + plain(fwd, bwd),
        [unit_out, unit_out, unit_out, loss_out], [z_vmem], flops,
    )
    last = swap(odd_high_second.reshape(16, 32, N))
    half_block = pl.BlockSpec((GROUP * 2 * N, 2 * N), lambda i: (i, 0))
    half_out = ((16 * 2 * N, 2 * N), bf16, half_block)
    start, sums, high, low = run(
        even_out, 16 // GROUP,
        small(rows, off_even, beta) + plain(ahead, from_left, mid, loss_a, loss_b, loss_c, probe)
        + [(amp_even, pl.BlockSpec((GROUP, N, N), lambda i: (i, 0, 0)))] + plain(fwd),
        [unit_out, loss_out, half_out, half_out], [pltpu.VMEM((8, N), f32), z_vmem], flops // 2,
    )
    (send,) = small_call(
        pass_last, small(left) + [(last, VMEM), (sums, VMEM)], [((16, 40, N), f32, VMEM)]
    )
    got = swap(send)
    (tile,) = run(
        even_back, 16 // GROUP,
        small(rows, off_even) + plain(start, mid, odd_low_second, probe)
        + [(high, half_block), (low, half_block)] + plain(bwd),
        [((2, 256, 256), f32, None)], [unit_vmem, unit_vmem], flops // 2,
    )
    got, tile = lax.optimization_barrier((got, tile))
    sums = jnp.sum(got[:, 32:], axis=0)
    sums = swap(sums, "ty")
    left_block = pl.BlockSpec((2, 256, N), lambda i: (0, 0, 0))
    tile = pl.pallas_call(
        finish,
        grid=(1,),
        out_shape=jax.ShapeDtypeStruct((2, 256, 256), f32),
        in_specs=[left_block, pl.BlockSpec((16, 32, N), lambda i: (0, 0, 0))],
        out_specs=left_block,
        input_output_aliases={0: 0},
        compiler_params=pltpu.CompilerParams(vmem_limit_bytes=VMEM_BYTES),
    )(tile, got)
    losses = jnp.sum(jnp.sum(sums, axis=0).reshape(2, N // 2), axis=1) * (0.5 / 67108864.0)
    return (tile, losses)


def solution(mesh):
    in_specs = (
        P(None, "ty", "tx"),
        P(None, "ty", "tx"),
        P(),
        P(("ty", "tx"), None, None, None),
        P(),
        P(("ty", "tx"), None),
        P(),
        P(),
    )
    return jax.shard_map(
        shards, mesh=mesh, in_specs=in_specs, out_specs=(P(None, "ty", "tx"), P()), check_vma=False
    )
```

```python
import functools
import math

import jax
import jax.numpy as jnp
import ml_dtypes
import numpy as np
from jax import lax
from jax.experimental import pallas as pl
from jax.experimental.pallas import tpu as pltpu
from jax.sharding import PartitionSpec as P

START = 100
STABILIZER = 0.05
STEP = 0.25
N = 128
GROUP = 8
VMEM_BYTES = 60 * 2**20
f32 = jnp.float32
bf16 = jnp.bfloat16
SMEM = pl.BlockSpec(memory_space=pltpu.SMEM)
VMEM = pl.BlockSpec(memory_space=pltpu.VMEM)
ANY = pl.BlockSpec(memory_space=pl.ANY)
HBM = pl.BlockSpec(memory_space=pltpu.HBM)


def momentum_table():
    values = [1.0]
    for counter in range(START):
        last = values[-1]
        values.append((1.0 + (1.0 + 4.0 * last * last) ** 0.5) / 2.0)
    return jnp.asarray(values, f32)


def dft_tables():
    index = np.arange(N)
    angle = (index[:, None] * index[None, :] % N).astype(np.float64) * (2.0 * math.pi / N)
    cos, sin = np.cos(angle) / math.sqrt(N), np.sin(angle) / math.sqrt(N)

    def stacked(table):
        high = table.astype(ml_dtypes.bfloat16)
        low = (table - high.astype(np.float64)).astype(ml_dtypes.bfloat16)
        return jnp.asarray(np.concatenate([high, high, low], 0))

    return stacked(np.block([[cos, -sin], [sin, cos]])), stacked(np.block([[cos, sin], [-sin, cos]]))


def times_table(block, table):
    parts = []
    for at in range(0, GROUP * 2 * N, N):
        if isinstance(block, tuple):
            high, low = block[0][at : at + N], block[1][at : at + N]
        else:
            part = block[at : at + N]
            high = part.astype(bf16)
            low = (part - high.astype(f32)).astype(bf16)
        parts.append(jnp.dot(jnp.concatenate([high, low, high], 1), table, preferred_element_type=f32))
    return jnp.concatenate(parts, 0)


def flip_blocks(block):
    rows = []
    for at in range(0, block.shape[0], N):
        rows.append(jnp.concatenate([block[at : at + N, :N].T, block[at : at + N, N:].T], 1))
    return jnp.concatenate(rows, 0)


def way_out(rows, offs, z, probe, amp, amp_first, fwd, loss, first):
    lane = lax.broadcasted_iota(jnp.int32, (N, N), 1)
    waves = []
    for u in range(GROUP):
        top, off = rows[first + u], offs[first + u]
        inside = lane >= off
        patch = [
            pltpu.roll(jnp.where(inside, z[0, k, pl.ds(top, N), :], z[1, k, pl.ds(top, N), :]), (N - off) & (N - 1), 1)
            for k in range(2)
        ]
        for m in range(2):
            re, im = probe[m, 0], probe[m, 1]
            waves.append(jnp.concatenate([re * patch[0] - im * patch[1], re * patch[1] + im * patch[0]], 1))
    wave = times_table(flip_blocks(times_table(jnp.concatenate(waves, 0), fwd[...])), fwd[...])
    weighted = []
    total = jnp.zeros((8, N), f32)
    for u in range(GROUP):
        w = wave[u * 2 * N : (u + 1) * 2 * N]
        square = w * w
        square = square[:N] + square[N:]
        square = square[:, :N] + square[:, N:] + STABILIZER
        inverse = lax.rsqrt(square)
        measured = amp[amp_first + u].T
        miss = square * inverse - measured
        total = total + jnp.sum((miss * miss).reshape(N // 8, 8, N), 0)
        weight = 1.0 - measured * inverse
        weight = jnp.concatenate([weight, weight], 1)
        weighted += [weight * w[:N], weight * w[N:]]
    loss[...] += total
    return jnp.concatenate(weighted, 0)


def way_back(rows, offs, probe, weighted, bwd, left, right, first):
    lane = lax.broadcasted_iota(jnp.int32, (N, N), 1)
    back = times_table(flip_blocks(times_table(weighted, bwd[...])), bwd[...])
    for u in range(GROUP):
        top, off = rows[first + u], offs[first + u]
        inside = lane >= off
        grad_re, grad_im = 0.0, 0.0
        for m in range(2):
            re, im = probe[m, 0], probe[m, 1]
            b = back[(2 * u + m) * N : (2 * u + m + 1) * N]
            grad_re = grad_re + re * b[:, :N] + im * b[:, N:]
            grad_im = grad_im + re * b[:, N:] - im * b[:, :N]
        for k, grad in ((0, grad_re), (1, grad_im)):
            moved = pltpu.roll(grad, off, 1)
            left[k, pl.ds(top, N), :] += jnp.where(inside, moved, 0.0)
            right[k, pl.ds(top, N), :] += jnp.where(inside, 0.0, moved)


def all_positions(rows, offs, z, probe, amp, fwd, bwd, left, right, loss):
    clear(left, right, loss)

    def group(g, carry):
        first = g * GROUP
        weighted = way_out(rows, offs, z, probe, amp, first, fwd, loss, first)
        way_back(rows, offs, probe, weighted, bwd, left, right, first)
        return carry

    lax.fori_loop(0, 16 // GROUP, group, 0)


def clear(*refs):
    for ref in refs:
        ref[...] = jnp.zeros_like(ref)


def unit(tile, k, u):
    return tile[k, :, u * N : (u + 1) * N]


def chunk_of(ref, d):
    return ref.at[d // 8, pl.ds(32 * (d % 8), 32)]


def even_first(rows, offs, beta, obj, prev, probe, amp, fwd, bwd, z0, even_low, even_high, ahead, loss):
    for u in range(2):
        for k in range(2):
            now = unit(obj, k, u)
            z0[u, k] = now + beta[0] * (now - unit(prev, k, u))
    all_positions(rows, offs, z0, probe, amp, fwd, bwd, even_low, even_high, loss)
    b = beta[1]
    for k in range(2):
        ahead[k] = (1.0 + b) * (z0[0, k] - STEP * even_low[k]) - b * unit(obj, k, 0)


def odd_first(rows, offs, z0, halo, probe, amp, fwd, bwd, odd_low, odd_high, loss, z):
    z[0] = z0[0]
    for d in range(16):
        chunk_of(z.at[1], d)[...] = halo[d]
    all_positions(rows, offs, z, probe, amp, fwd, bwd, odd_low, odd_high, loss)


def odd_second(
    rows, offs, beta, z0, obj, even_high, odd_low, odd_high, ahead, probe, amp, fwd, bwd,
    mid, low_second, high_second, loss, z,
):
    b = beta[1]
    scale = (1.0 + b) * STEP
    for k in range(2):
        now = z0[0, k] - STEP * (even_high[k] + odd_low[k])
        mid[k] = now + b * (now - obj[k])
        z[0, k] = mid[k]
    for d in range(16):
        chunk_of(z.at[1], d)[...] = ahead[d, :32] - scale * chunk_of(odd_high, d)[...]
    all_positions(rows, offs, z, probe, amp, fwd, bwd, low_second, high_second, loss)


def even_out(rows, offs, beta, ahead, from_left, mid, loss_a, loss_b, loss_c, probe, amp, fwd, start, sums, high, low, loss, z):
    @pl.when(pl.program_id(0) == 0)
    def _():
        clear(loss)
        scale = (1.0 + beta[1]) * STEP
        for d in range(16):
            chunk_of(z.at[0], d)[...] = chunk_of(ahead, d)[...] - scale * from_left[d]
        z[1] = mid[...]
        start[...] = z[0]

    weighted = way_out(rows, offs, z, probe, amp, 0, fwd, loss, pl.program_id(0) * GROUP)
    high[...] = weighted.astype(bf16)
    low[...] = (weighted - high[...].astype(f32)).astype(bf16)

    @pl.when(pl.program_id(0) == pl.num_programs(0) - 1)
    def _():
        whole = lambda x: jnp.sum(jnp.sum(x, axis=0, keepdims=True), axis=1, keepdims=True)
        lane = lax.broadcasted_iota(jnp.int32, (32, N), 1)
        line = lax.broadcasted_iota(jnp.int32, (32, N), 0)
        both = jnp.where(line < 16, whole(loss_a[...] + loss_b[...]), whole(loss_c[...] + loss[...]))
        sums[...] = jnp.where(lane == N - 1, both, 0.0)


def even_back(rows, offs, start, mid, odd_low, probe, high, low, bwd, tile, even_low, even_high):
    @pl.when(pl.program_id(0) == 0)
    def _():
        clear(even_low, even_high)

    way_back(rows, offs, probe, (high, low), bwd, even_low, even_high, pl.program_id(0) * GROUP)

    @pl.when(pl.program_id(0) == pl.num_programs(0) - 1)
    def _():
        for k in range(2):
            tile[k, :, :N] = start[k] - STEP * even_low[k]
            tile[k, :, N:] = mid[k] - STEP * (even_high[k] + odd_low[k])


def run(kernel, steps, args, outs, scratch, flops, limit=VMEM_BYTES):
    whole = lambda a: pl.BlockSpec(a.shape, lambda i, n=len(a.shape): (0,) * n)
    out_shape = [jax.ShapeDtypeStruct(s, d) for s, d, _ in outs]
    return pl.pallas_call(
        kernel,
        grid=(steps,),
        out_shape=out_shape,
        in_specs=[spec or whole(a) for a, spec in args],
        out_specs=[spec or whole(o) for o, (_, _, spec) in zip(out_shape, outs)],
        scratch_shapes=scratch,
        compiler_params=pltpu.CompilerParams(vmem_limit_bytes=limit),
        cost_estimate=pl.CostEstimate(flops=flops, bytes_accessed=2**22, transcendentals=0),
    )(*[a for a, _ in args])


def small_call(kernel, args, outs, scratch=(), limit=6 * 2**20):
    return pl.pallas_call(
        kernel,
        out_shape=[jax.ShapeDtypeStruct(s, d) for s, d, _ in outs],
        in_specs=[spec for _, spec in args],
        out_specs=[spec for _, _, spec in outs],
        scratch_shapes=list(scratch),
        compiler_params=pltpu.CompilerParams(vmem_limit_bytes=limit),
    )(*[a for a, _ in args])


def start_all(pairs, sems):
    copies = [pltpu.make_async_copy(a, b, sems.at[i]) for i, (a, b) in enumerate(pairs)]
    for c in copies:
        c.start()
    return copies


def prepare(
    owner_map, row_tops, restart, table, cols, obj, prev, amp, send, rows, inv, right, left, beta, now, before, sems
):
    edges = start_all([(obj.at[:, :, pl.ds(0, N)], now), (prev.at[:, :, pl.ds(0, N)], before)], sems.at[pl.ds(16, 2)])
    band = lax.axis_index("ty")
    for c in range(16):
        owner = owner_map[band, c]
        inv[owner] = c
        right[owner] = owner_map[band, (c + 1) % 16]
        left[owner] = owner_map[band, (c + 15) % 16]
        rows[c] = row_tops[band * 16 + c]
    copies = start_all([(amp.at[2 * inv[d]], send.at[d, pl.ds(0, N)]) for d in range(16)], sems)
    for k in range(2):
        beta[k] = (table[restart[k] - 1] - 1.0) / table[restart[k]]
    for c in edges:
        c.wait()
    now[...] = now[...] + beta[0] * (now[...] - before[...])
    lane = lax.broadcasted_iota(jnp.int32, (32, N), 1)
    line = lax.broadcasted_iota(jnp.int32, (32, N), 0)
    for d in range(16):
        col = inv[d]
        even = cols[0, 2 * col] - 2 * N * col
        odd = cols[0, 2 * col + 1] - 2 * N * col - N
        places = jnp.where(line == 0, even, odd).astype(f32)
        send[d, N:] = jnp.where(lane == N - 1, places, chunk_of(now, d)[...])
    for c in copies:
        c.wait()


def pass_halo(right, inv, got, amp, send, off_even, off_odd, places, sems):
    fetch_places = pltpu.make_async_copy(got.at[:, pl.ds(N, 2)], places, sems.at[32])
    fetch_places.start()
    copies = start_all(
        [(amp.at[2 * inv[d] + 1], send.at[d, pl.ds(0, N)]) for d in range(16)]
        + [(got.at[right[d], pl.ds(N, 32)], send.at[d, pl.ds(N, 32)]) for d in range(16)],
        sems,
    )
    fetch_places.wait()
    for r in range(16):
        off_even[r] = places[r, 0, N - 1].astype(jnp.int32)
        off_odd[r] = places[r, 1, N - 1].astype(jnp.int32)
    for c in copies:
        c.wait()


def pass_ahead(right, ahead, odd_high, send, edge, sem):
    fetch = pltpu.make_async_copy(odd_high, edge, sem)
    fetch.start()
    for d in range(16):
        send[d, :32] = ahead[right[d]]
    fetch.wait()
    for d in range(16):
        send[d, 32:] = chunk_of(edge, d)[...]


def pass_left(left, got, send):
    for d in range(16):
        send[d] = got[left[d], 32:]


def pass_last(left, got, sums, send):
    for d in range(16):
        send[d] = got[left[d]] + sums[...]


def finish(tile, got, out):
    edge = lax.broadcasted_iota(jnp.int32, (32, N), 1) < N - 1
    for d in range(16):
        at = pl.ds(32 * (d % 8), 32)
        out[d // 8, at] = tile[d // 8, at] - STEP * jnp.where(edge, got[d], 0.0)


def swap(block, axis="tx"):
    return lax.all_to_all(block, axis, 0, 0, tiled=True)


def shards(obj, prev, probe, amplitude, row_tops, scan_cols, restart, owner_map):
    fwd, bwd = dft_tables()
    ints = ((16,), jnp.int32, SMEM)
    unit_out, loss_out = ((2, 256, N), f32, None), ((8, N), f32, None)
    z_vmem = pltpu.VMEM((2, 2, 256, N), f32)
    unit_vmem = pltpu.VMEM((2, 256, N), f32)
    images = pl.BlockSpec((16, N, N), lambda i: (0, 0, 0))
    right_unit = pl.BlockSpec((1, 2, 256, N), lambda i: (1, 0, 0, 0))
    edge = pl.BlockSpec((16, 32, N), lambda i: (0, N // 32, 0))
    plain = lambda *arrays: [(a, None) for a in arrays]
    small = lambda *arrays: [(a, SMEM) for a in arrays]
    flops = 16 * 400_000_000

    amplitude = amplitude[0]
    send, rows, inv, right, left, beta = small_call(
        prepare,
        small(owner_map, row_tops, restart, momentum_table(), scan_cols)
        + [(obj, ANY), (prev, ANY), (amplitude, ANY)],
        [((16, N + 32, N), f32, VMEM), ints, ints, ints, ints, ((2,), f32, SMEM)],
        [unit_vmem, unit_vmem, pltpu.SemaphoreType.DMA((18,))], limit=VMEM_BYTES,
    )
    amp_even = swap(send)
    send, off_even, off_odd = small_call(
        pass_halo, small(right, inv) + [(amp_even, ANY), (amplitude, ANY)],
        [((16, N + 32, N), f32, VMEM), ints, ints],
        [pltpu.SMEM((16, 2, N), f32), pltpu.SemaphoreType.DMA((33,))], limit=VMEM_BYTES,
    )
    amp_odd = swap(send)
    z0, even_low, even_high, ahead, loss_a = run(
        even_first, 1, small(rows, off_even, beta) + plain(obj, prev, probe) + [(amp_even, images)] + plain(fwd, bwd),
        [((2, 2, 256, N), f32, None), unit_out, unit_out, unit_out, loss_out], [], flops,
    )
    got = swap(ahead.reshape(16, 32, N))
    odd_low, odd_high, loss_b = run(
        odd_first, 1,
        small(rows, off_odd) + [(z0, right_unit), (amp_odd, edge)] + plain(probe) + [(amp_odd, images)] + plain(fwd, bwd),
        [unit_out, unit_out, loss_out], [z_vmem], flops,
    )
    (send,) = small_call(
        pass_ahead, small(right) + [(got, VMEM), (odd_high, HBM)], [((16, 64, N), f32, VMEM)],
        [unit_vmem, pltpu.SemaphoreType.DMA(())],
    )
    got = swap(send)
    (send,) = small_call(pass_left, small(left) + [(got, VMEM)], [((16, 32, N), f32, VMEM)])
    from_left = swap(send)
    mid, odd_low_second, odd_high_second, loss_c = run(
        odd_second, 1,
        small(rows, off_odd, beta) + [(z0, right_unit), (obj, pl.BlockSpec((2, 256, N), lambda i: (0, 0, 1)))]
        + plain(even_high, odd_low, odd_high, got, probe)
        + [(amp_odd, images)] + plain(fwd, bwd),
        [unit_out, unit_out, unit_out, loss_out], [z_vmem], flops,
    )
    last = swap(odd_high_second.reshape(16, 32, N))
    half_block = pl.BlockSpec((GROUP * 2 * N, 2 * N), lambda i: (i, 0))
    half_out = ((16 * 2 * N, 2 * N), bf16, half_block)
    start, sums, high, low = run(
        even_out, 16 // GROUP,
        small(rows, off_even, beta) + plain(ahead, from_left, mid, loss_a, loss_b, loss_c, probe)
        + [(amp_even, pl.BlockSpec((GROUP, N, N), lambda i: (i, 0, 0)))] + plain(fwd),
        [unit_out, ((32, N), f32, None), half_out, half_out], [pltpu.VMEM((8, N), f32), z_vmem], flops // 2,
    )
    (send,) = small_call(
        pass_last, small(left) + [(last, VMEM), (sums, VMEM)], [((16, 32, N), f32, VMEM)]
    )
    got = swap(send)
    (tile,) = run(
        even_back, 16 // GROUP,
        small(rows, off_even) + plain(start, mid, odd_low_second, probe)
        + [(high, half_block), (low, half_block)] + plain(bwd),
        [((2, 256, 256), f32, None)], [unit_vmem, unit_vmem], flops // 2,
    )
    got, tile = lax.optimization_barrier((got, tile))
    sums = jnp.broadcast_to(jnp.tile(jnp.sum(got[:, :, N - 1], axis=0), 4), (8, N))
    sums = swap(sums, "ty")
    left_block = pl.BlockSpec((2, 256, N), lambda i: (0, 0, 0))
    tile = pl.pallas_call(
        finish,
        grid=(1,),
        out_shape=jax.ShapeDtypeStruct((2, 256, 256), f32),
        in_specs=[left_block, pl.BlockSpec((16, 32, N), lambda i: (0, 0, 0))],
        out_specs=left_block,
        input_output_aliases={0: 0},
        compiler_params=pltpu.CompilerParams(vmem_limit_bytes=VMEM_BYTES),
    )(tile, got)
    losses = jnp.sum(sums, axis=0)[: 32 : 16] * (0.5 / 67108864.0)
    return (tile, losses)


def solution(mesh):
    in_specs = (
        P(None, "ty", "tx"),
        P(None, "ty", "tx"),
        P(),
        P(("ty", "tx"), None, None, None),
        P(),
        P(("ty", "tx"), None),
        P(),
        P(),
    )
    return jax.shard_map(
        shards, mesh=mesh, in_specs=in_specs, out_specs=(P(None, "ty", "tx"), P()), check_vma=False
    )
```

```python
import functools
import math

import jax
import jax.numpy as jnp
import ml_dtypes
import numpy as np
from jax import lax
from jax.experimental import pallas as pl
from jax.experimental.pallas import tpu as pltpu
from jax.sharding import PartitionSpec as P

START = 100
STABILIZER = 0.05
STEP = 0.25
N = 128
GROUP = 8
VMEM_BYTES = 60 * 2**20
f32 = jnp.float32
bf16 = jnp.bfloat16
SMEM = pl.BlockSpec(memory_space=pltpu.SMEM)
VMEM = pl.BlockSpec(memory_space=pltpu.VMEM)
ANY = pl.BlockSpec(memory_space=pl.ANY)
HBM = pl.BlockSpec(memory_space=pltpu.HBM)


def momentum_table():
    values = [1.0]
    for counter in range(START):
        last = values[-1]
        values.append((1.0 + (1.0 + 4.0 * last * last) ** 0.5) / 2.0)
    return jnp.asarray(values, f32)


def dft_tables():
    index = np.arange(N)
    angle = (index[:, None] * index[None, :] % N).astype(np.float64) * (2.0 * math.pi / N)
    cos, sin = np.cos(angle) / math.sqrt(N), np.sin(angle) / math.sqrt(N)

    def stacked(table):
        high = table.astype(ml_dtypes.bfloat16)
        low = (table - high.astype(np.float64)).astype(ml_dtypes.bfloat16)
        return jnp.asarray(np.concatenate([high, high, low], 0))

    return stacked(np.block([[cos, -sin], [sin, cos]])), stacked(np.block([[cos, sin], [-sin, cos]]))


def times_table(block, table):
    parts = []
    for at in range(0, GROUP * 2 * N, N):
        if isinstance(block, tuple):
            high, low = block[0][at : at + N], block[1][at : at + N]
        else:
            part = block[at : at + N]
            high = part.astype(bf16)
            low = (part - high.astype(f32)).astype(bf16)
        parts.append(jnp.dot(jnp.concatenate([high, low, high], 1), table, preferred_element_type=f32))
    return jnp.concatenate(parts, 0)


def flip_blocks(block):
    rows = []
    for at in range(0, block.shape[0], N):
        rows.append(jnp.concatenate([block[at : at + N, :N].T, block[at : at + N, N:].T], 1))
    return jnp.concatenate(rows, 0)


def way_out(rows, offs, z, probe, amp, amp_first, fwd, loss, first):
    lane = lax.broadcasted_iota(jnp.int32, (N, N), 1)
    waves = []
    for u in range(GROUP):
        top, off = rows[first + u], offs[first + u]
        inside = lane >= off
        patch = [
            pltpu.roll(jnp.where(inside, z[0, k, pl.ds(top, N), :], z[1, k, pl.ds(top, N), :]), (N - off) & (N - 1), 1)
            for k in range(2)
        ]
        for m in range(2):
            re, im = probe[m, 0], probe[m, 1]
            waves.append(jnp.concatenate([re * patch[0] - im * patch[1], re * patch[1] + im * patch[0]], 1))
    wave = times_table(flip_blocks(times_table(jnp.concatenate(waves, 0), fwd[...])), fwd[...])
    weighted = []
    total = jnp.zeros((8, N), f32)
    for u in range(GROUP):
        w = wave[u * 2 * N : (u + 1) * 2 * N]
        square = w * w
        square = square[:N] + square[N:]
        square = square[:, :N] + square[:, N:] + STABILIZER
        inverse = lax.rsqrt(square)
        measured = amp[amp_first + u].T
        miss = square * inverse - measured
        total = total + jnp.sum((miss * miss).reshape(N // 8, 8, N), 0)
        weight = 1.0 - measured * inverse
        weight = jnp.concatenate([weight, weight], 1)
        weighted += [weight * w[:N], weight * w[N:]]
    loss[...] += total
    return jnp.concatenate(weighted, 0)


def way_back(rows, offs, probe, weighted, bwd, left, right, first):
    lane = lax.broadcasted_iota(jnp.int32, (N, N), 1)
    back = times_table(flip_blocks(times_table(weighted, bwd[...])), bwd[...])
    for u in range(GROUP):
        top, off = rows[first + u], offs[first + u]
        inside = lane >= off
        grad_re, grad_im = 0.0, 0.0
        for m in range(2):
            re, im = probe[m, 0], probe[m, 1]
            b = back[(2 * u + m) * N : (2 * u + m + 1) * N]
            grad_re = grad_re + re * b[:, :N] + im * b[:, N:]
            grad_im = grad_im + re * b[:, N:] - im * b[:, :N]
        for k, grad in ((0, grad_re), (1, grad_im)):
            moved = pltpu.roll(grad, off, 1)
            left[k, pl.ds(top, N), :] += jnp.where(inside, moved, 0.0)
            right[k, pl.ds(top, N), :] += jnp.where(inside, 0.0, moved)


def all_positions(rows, offs, z, probe, amp, fwd, bwd, left, right, loss):
    clear(left, right, loss)

    def group(g, carry):
        first = g * GROUP
        weighted = way_out(rows, offs, z, probe, amp, first, fwd, loss, first)
        way_back(rows, offs, probe, weighted, bwd, left, right, first)
        return carry

    lax.fori_loop(0, 16 // GROUP, group, 0)


def clear(*refs):
    for ref in refs:
        ref[...] = jnp.zeros_like(ref)


def unit(tile, k, u):
    return tile[k, :, u * N : (u + 1) * N]


def chunk_of(ref, d):
    return ref.at[d // 8, pl.ds(32 * (d % 8), 32)]


def even_first(rows, offs, beta, obj, prev, probe, amp, fwd, bwd, z0, even_low, even_high, ahead, loss):
    for u in range(2):
        for k in range(2):
            now = unit(obj, k, u)
            z0[u, k] = now + beta[0] * (now - unit(prev, k, u))
    all_positions(rows, offs, z0, probe, amp, fwd, bwd, even_low, even_high, loss)
    b = beta[1]
    for k in range(2):
        ahead[k] = (1.0 + b) * (z0[0, k] - STEP * even_low[k]) - b * unit(obj, k, 0)


def odd_first(rows, offs, z0, halo, probe, amp, fwd, bwd, odd_low, odd_high, loss, z):
    z[0] = z0[0]
    for d in range(16):
        chunk_of(z.at[1], d)[...] = halo[d]
    all_positions(rows, offs, z, probe, amp, fwd, bwd, odd_low, odd_high, loss)


def odd_second(
    rows, offs, beta, z0, obj, even_high, odd_low, odd_high, ahead, probe, amp, fwd, bwd,
    mid, low_second, high_second, loss, z,
):
    b = beta[1]
    scale = (1.0 + b) * STEP
    for k in range(2):
        now = z0[0, k] - STEP * (even_high[k] + odd_low[k])
        mid[k] = now + b * (now - obj[k])
        z[0, k] = mid[k]
    for d in range(16):
        chunk_of(z.at[1], d)[...] = ahead[d, :32] - scale * chunk_of(odd_high, d)[...]
    all_positions(rows, offs, z, probe, amp, fwd, bwd, low_second, high_second, loss)


def even_out(rows, offs, beta, ahead, from_left, mid, loss_a, loss_b, loss_c, probe, amp, fwd, start, sums, high, low, loss, z):
    @pl.when(pl.program_id(0) == 0)
    def _():
        clear(loss)
        scale = (1.0 + beta[1]) * STEP
        for d in range(16):
            chunk_of(z.at[0], d)[...] = chunk_of(ahead, d)[...] - scale * from_left[d]
        z[1] = mid[...]
        start[...] = z[0]

    weighted = way_out(rows, offs, z, probe, amp, 0, fwd, loss, pl.program_id(0) * GROUP)
    high[...] = weighted.astype(bf16)
    low[...] = (weighted - high[...].astype(f32)).astype(bf16)

    @pl.when(pl.program_id(0) == pl.num_programs(0) - 1)
    def _():
        whole = lambda x: jnp.sum(jnp.sum(x, axis=0, keepdims=True), axis=1, keepdims=True)
        lane = lax.broadcasted_iota(jnp.int32, (32, N), 1)
        line = lax.broadcasted_iota(jnp.int32, (32, N), 0)
        both = jnp.where(line < 16, whole(loss_a[...] + loss_b[...]), whole(loss_c[...] + loss[...]))
        sums[...] = jnp.where(lane == N - 1, both, 0.0)


def even_back(rows, offs, start, mid, odd_low, probe, high, low, bwd, tile, even_low, even_high):
    @pl.when(pl.program_id(0) == 0)
    def _():
        clear(even_low, even_high)

    way_back(rows, offs, probe, (high, low), bwd, even_low, even_high, pl.program_id(0) * GROUP)

    @pl.when(pl.program_id(0) == pl.num_programs(0) - 1)
    def _():
        for k in range(2):
            tile[k, :, :N] = start[k] - STEP * even_low[k]
            tile[k, :, N:] = mid[k] - STEP * (even_high[k] + odd_low[k])


def run(kernel, steps, args, outs, scratch, flops, limit=VMEM_BYTES):
    whole = lambda a: pl.BlockSpec(a.shape, lambda i, n=len(a.shape): (0,) * n)
    out_shape = [jax.ShapeDtypeStruct(s, d) for s, d, _ in outs]
    return pl.pallas_call(
        kernel,
        grid=(steps,),
        out_shape=out_shape,
        in_specs=[spec or whole(a) for a, spec in args],
        out_specs=[spec or whole(o) for o, (_, _, spec) in zip(out_shape, outs)],
        scratch_shapes=scratch,
        compiler_params=pltpu.CompilerParams(vmem_limit_bytes=limit),
        cost_estimate=pl.CostEstimate(flops=flops, bytes_accessed=2**22, transcendentals=0),
    )(*[a for a, _ in args])


def small_call(kernel, args, outs, scratch=(), limit=6 * 2**20):
    return pl.pallas_call(
        kernel,
        out_shape=[jax.ShapeDtypeStruct(s, d) for s, d, _ in outs],
        in_specs=[spec for _, spec in args],
        out_specs=[spec for _, _, spec in outs],
        scratch_shapes=list(scratch),
        compiler_params=pltpu.CompilerParams(vmem_limit_bytes=limit),
    )(*[a for a, _ in args])


def start_all(pairs, sems):
    copies = [pltpu.make_async_copy(a, b, sems.at[i]) for i, (a, b) in enumerate(pairs)]
    for c in copies:
        c.start()
    return copies


def prepare(
    owner_map, row_tops, restart, table, cols, obj, prev, amp, send, rows, inv, right, left, beta, now, before, sems
):
    edges = start_all([(obj.at[:, :, pl.ds(0, N)], now), (prev.at[:, :, pl.ds(0, N)], before)], sems.at[pl.ds(16, 2)])
    band = lax.axis_index("ty")
    for c in range(16):
        owner = owner_map[band, c]
        inv[owner] = c
        right[owner] = owner_map[band, (c + 1) % 16]
        left[owner] = owner_map[band, (c + 15) % 16]
        rows[c] = row_tops[band * 16 + c]
    copies = start_all([(amp.at[2 * inv[d]], send.at[d, pl.ds(0, N)]) for d in range(16)], sems)
    for k in range(2):
        beta[k] = (table[restart[k] - 1] - 1.0) / table[restart[k]]
    for c in edges:
        c.wait()
    now[...] = now[...] + beta[0] * (now[...] - before[...])
    lane = lax.broadcasted_iota(jnp.int32, (32, N), 1)
    line = lax.broadcasted_iota(jnp.int32, (32, N), 0)
    for d in range(16):
        col = inv[d]
        even = cols[0, 2 * col] - 2 * N * col
        odd = cols[0, 2 * col + 1] - 2 * N * col - N
        places = jnp.where(line == 0, even, odd).astype(f32)
        send[d, N:] = jnp.where(lane == N - 1, places, chunk_of(now, d)[...])
    for c in copies:
        c.wait()


def pass_halo(right, inv, got, amp, send, off_even, off_odd, places, edges, sems):
    fetch_edges = pltpu.make_async_copy(got.at[:, pl.ds(N, 32)], edges, sems.at[16])
    fetch_places = pltpu.make_async_copy(got.at[:, pl.ds(N, 2)], places, sems.at[17])
    fetch_edges.start()
    fetch_places.start()
    copies = start_all([(amp.at[2 * inv[d] + 1], send.at[d, pl.ds(0, N)]) for d in range(16)], sems)
    fetch_edges.wait()
    for d in range(16):
        send[d, N:] = edges[right[d]]
    fetch_places.wait()
    for r in range(16):
        off_even[r] = places[r, 0, N - 1].astype(jnp.int32)
        off_odd[r] = places[r, 1, N - 1].astype(jnp.int32)
    for c in copies:
        c.wait()


def pass_ahead(right, ahead, odd_high, send, edge, sem):
    fetch = pltpu.make_async_copy(odd_high, edge, sem)
    fetch.start()
    for d in range(16):
        send[d, :32] = ahead[right[d]]
    fetch.wait()
    for d in range(16):
        send[d, 32:] = chunk_of(edge, d)[...]


def pass_left(left, got, send):
    for d in range(16):
        send[d] = got[left[d], 32:]


def pass_last(left, got, sums, send):
    for d in range(16):
        send[d] = got[left[d]] + sums[...]


def finish(tile, got, out):
    edge = lax.broadcasted_iota(jnp.int32, (32, N), 1) < N - 1
    for d in range(16):
        at = pl.ds(32 * (d % 8), 32)
        out[d // 8, at] = tile[d // 8, at] - STEP * jnp.where(edge, got[d], 0.0)


def swap(block, axis="tx"):
    return lax.all_to_all(block, axis, 0, 0, tiled=True)


def shards(obj, prev, probe, amplitude, row_tops, scan_cols, restart, owner_map):
    fwd, bwd = dft_tables()
    ints = ((16,), jnp.int32, SMEM)
    unit_out, loss_out = ((2, 256, N), f32, None), ((8, N), f32, None)
    z_vmem = pltpu.VMEM((2, 2, 256, N), f32)
    unit_vmem = pltpu.VMEM((2, 256, N), f32)
    images = pl.BlockSpec((16, N, N), lambda i: (0, 0, 0))
    right_unit = pl.BlockSpec((1, 2, 256, N), lambda i: (1, 0, 0, 0))
    edge = pl.BlockSpec((16, 32, N), lambda i: (0, N // 32, 0))
    plain = lambda *arrays: [(a, None) for a in arrays]
    small = lambda *arrays: [(a, SMEM) for a in arrays]
    flops = 16 * 400_000_000

    amplitude = amplitude[0]
    send, rows, inv, right, left, beta = small_call(
        prepare,
        small(owner_map, row_tops, restart, momentum_table(), scan_cols)
        + [(obj, ANY), (prev, ANY), (amplitude, ANY)],
        [((16, N + 32, N), f32, VMEM), ints, ints, ints, ints, ((2,), f32, SMEM)],
        [unit_vmem, unit_vmem, pltpu.SemaphoreType.DMA((18,))], limit=VMEM_BYTES,
    )
    amp_even = swap(send)
    send, off_even, off_odd = small_call(
        pass_halo, small(right, inv) + [(amp_even, ANY), (amplitude, ANY)],
        [((16, N + 32, N), f32, VMEM), ints, ints],
        [pltpu.SMEM((16, 2, N), f32), pltpu.VMEM((16, 32, N), f32), pltpu.SemaphoreType.DMA((18,))], limit=VMEM_BYTES,
    )
    amp_odd = swap(send)
    z0, even_low, even_high, ahead, loss_a = run(
        even_first, 1, small(rows, off_even, beta) + plain(obj, prev, probe) + [(amp_even, images)] + plain(fwd, bwd),
        [((2, 2, 256, N), f32, None), unit_out, unit_out, unit_out, loss_out], [], flops,
    )
    got = swap(ahead.reshape(16, 32, N))
    odd_low, odd_high, loss_b = run(
        odd_first, 1,
        small(rows, off_odd) + [(z0, right_unit), (amp_odd, edge)] + plain(probe) + [(amp_odd, images)] + plain(fwd, bwd),
        [unit_out, unit_out, loss_out], [z_vmem], flops,
    )
    (send,) = small_call(
        pass_ahead, small(right) + [(got, VMEM), (odd_high, HBM)], [((16, 64, N), f32, VMEM)],
        [unit_vmem, pltpu.SemaphoreType.DMA(())],
    )
    got = swap(send)
    (send,) = small_call(pass_left, small(left) + [(got, VMEM)], [((16, 32, N), f32, VMEM)])
    from_left = swap(send)
    mid, odd_low_second, odd_high_second, loss_c = run(
        odd_second, 1,
        small(rows, off_odd, beta) + [(z0, right_unit), (obj, pl.BlockSpec((2, 256, N), lambda i: (0, 0, 1)))]
        + plain(even_high, odd_low, odd_high, got, probe)
        + [(amp_odd, images)] + plain(fwd, bwd),
        [unit_out, unit_out, unit_out, loss_out], [z_vmem], flops,
    )
    last = swap(odd_high_second.reshape(16, 32, N))
    half_block = pl.BlockSpec((GROUP * 2 * N, 2 * N), lambda i: (i, 0))
    half_out = ((16 * 2 * N, 2 * N), bf16, half_block)
    start, sums, high, low = run(
        even_out, 16 // GROUP,
        small(rows, off_even, beta) + plain(ahead, from_left, mid, loss_a, loss_b, loss_c, probe)
        + [(amp_even, pl.BlockSpec((GROUP, N, N), lambda i: (i, 0, 0)))] + plain(fwd),
        [unit_out, ((32, N), f32, None), half_out, half_out], [pltpu.VMEM((8, N), f32), z_vmem], flops // 2,
    )
    (send,) = small_call(
        pass_last, small(left) + [(last, VMEM), (sums, VMEM)], [((16, 32, N), f32, VMEM)]
    )
    got = swap(send)
    (tile,) = run(
        even_back, 16 // GROUP,
        small(rows, off_even) + plain(start, mid, odd_low_second, probe)
        + [(high, half_block), (low, half_block)] + plain(bwd),
        [((2, 256, 256), f32, None)], [unit_vmem, unit_vmem], flops // 2,
    )
    got, tile = lax.optimization_barrier((got, tile))
    sums = jnp.broadcast_to(jnp.tile(jnp.sum(got[:, :, N - 1], axis=0), 4), (8, N))
    sums = swap(sums, "ty")
    left_block = pl.BlockSpec((2, 256, N), lambda i: (0, 0, 0))
    tile = pl.pallas_call(
        finish,
        grid=(1,),
        out_shape=jax.ShapeDtypeStruct((2, 256, 256), f32),
        in_specs=[left_block, pl.BlockSpec((16, 32, N), lambda i: (0, 0, 0))],
        out_specs=left_block,
        input_output_aliases={0: 0},
        compiler_params=pltpu.CompilerParams(vmem_limit_bytes=VMEM_BYTES),
    )(tile, got)
    losses = jnp.sum(sums, axis=0)[: 32 : 16] * (0.5 / 67108864.0)
    return (tile, losses)


def solution(mesh):
    in_specs = (
        P(None, "ty", "tx"),
        P(None, "ty", "tx"),
        P(),
        P(("ty", "tx"), None, None, None),
        P(),
        P(("ty", "tx"), None),
        P(),
        P(),
    )
    return jax.shard_map(
        shards, mesh=mesh, in_specs=in_specs, out_specs=(P(None, "ty", "tx"), P()), check_vma=False
    )
```

```python
import functools
import math

import jax
import jax.numpy as jnp
import ml_dtypes
import numpy as np
from jax import lax
from jax.experimental import pallas as pl
from jax.experimental.pallas import tpu as pltpu
from jax.sharding import PartitionSpec as P

START = 100
STABILIZER = 0.05
STEP = 0.25
N = 128
GROUP = 8
VMEM_BYTES = 60 * 2**20
f32 = jnp.float32
bf16 = jnp.bfloat16
SMEM = pl.BlockSpec(memory_space=pltpu.SMEM)
VMEM = pl.BlockSpec(memory_space=pltpu.VMEM)
ANY = pl.BlockSpec(memory_space=pl.ANY)
HBM = pl.BlockSpec(memory_space=pltpu.HBM)


def momentum_table():
    values = [1.0]
    for counter in range(START):
        last = values[-1]
        values.append((1.0 + (1.0 + 4.0 * last * last) ** 0.5) / 2.0)
    return jnp.asarray(values, f32)


def dft_tables():
    index = np.arange(N)
    angle = (index[:, None] * index[None, :] % N).astype(np.float64) * (2.0 * math.pi / N)
    cos, sin = np.cos(angle) / math.sqrt(N), np.sin(angle) / math.sqrt(N)

    def stacked(table):
        high = table.astype(ml_dtypes.bfloat16)
        low = (table - high.astype(np.float64)).astype(ml_dtypes.bfloat16)
        return jnp.asarray(np.concatenate([high, high, low], 0))

    return stacked(np.block([[cos, -sin], [sin, cos]])), stacked(np.block([[cos, sin], [-sin, cos]]))


def times_table(block, table):
    parts = []
    for at in range(0, GROUP * 2 * N, N):
        if isinstance(block, tuple):
            high, low = block[0][at : at + N], block[1][at : at + N]
        else:
            part = block[at : at + N]
            high = part.astype(bf16)
            low = (part - high.astype(f32)).astype(bf16)
        parts.append(jnp.dot(jnp.concatenate([high, low, high], 1), table, preferred_element_type=f32))
    return jnp.concatenate(parts, 0)


def flip_blocks(block):
    rows = []
    for at in range(0, block.shape[0], N):
        rows.append(jnp.concatenate([block[at : at + N, :N].T, block[at : at + N, N:].T], 1))
    return jnp.concatenate(rows, 0)


def way_out(rows, offs, z, probe, amp, amp_first, fwd, loss, first):
    lane = lax.broadcasted_iota(jnp.int32, (N, N), 1)
    waves = []
    for u in range(GROUP):
        top, off = rows[first + u], offs[first + u]
        inside = lane >= off
        patch = [
            pltpu.roll(jnp.where(inside, z[0, k, pl.ds(top, N), :], z[1, k, pl.ds(top, N), :]), (N - off) & (N - 1), 1)
            for k in range(2)
        ]
        for m in range(2):
            re, im = probe[m, 0], probe[m, 1]
            waves.append(jnp.concatenate([re * patch[0] - im * patch[1], re * patch[1] + im * patch[0]], 1))
    wave = times_table(flip_blocks(times_table(jnp.concatenate(waves, 0), fwd[...])), fwd[...])
    weighted = []
    total = jnp.zeros((8, N), f32)
    for u in range(GROUP):
        w = wave[u * 2 * N : (u + 1) * 2 * N]
        square = w * w
        square = square[:N] + square[N:]
        square = square[:, :N] + square[:, N:] + STABILIZER
        inverse = lax.rsqrt(square)
        measured = amp[amp_first + u].T
        miss = square * inverse - measured
        total = total + jnp.sum((miss * miss).reshape(N // 8, 8, N), 0)
        weight = 1.0 - measured * inverse
        weight = jnp.concatenate([weight, weight], 1)
        weighted += [weight * w[:N], weight * w[N:]]
    loss[...] += total
    return jnp.concatenate(weighted, 0)


def way_back(rows, offs, probe, weighted, bwd, left, right, first):
    lane = lax.broadcasted_iota(jnp.int32, (N, N), 1)
    back = times_table(flip_blocks(times_table(weighted, bwd[...])), bwd[...])
    for u in range(GROUP):
        top, off = rows[first + u], offs[first + u]
        inside = lane >= off
        grad_re, grad_im = 0.0, 0.0
        for m in range(2):
            re, im = probe[m, 0], probe[m, 1]
            b = back[(2 * u + m) * N : (2 * u + m + 1) * N]
            grad_re = grad_re + re * b[:, :N] + im * b[:, N:]
            grad_im = grad_im + re * b[:, N:] - im * b[:, :N]
        for k, grad in ((0, grad_re), (1, grad_im)):
            moved = pltpu.roll(grad, off, 1)
            left[k, pl.ds(top, N), :] += jnp.where(inside, moved, 0.0)
            right[k, pl.ds(top, N), :] += jnp.where(inside, 0.0, moved)


def all_positions(rows, offs, z, probe, amp, fwd, bwd, left, right, loss):
    clear(left, right, loss)

    def group(g, carry):
        first = g * GROUP
        weighted = way_out(rows, offs, z, probe, amp, first, fwd, loss, first)
        way_back(rows, offs, probe, weighted, bwd, left, right, first)
        return carry

    lax.fori_loop(0, 16 // GROUP, group, 0)


def clear(*refs):
    for ref in refs:
        ref[...] = jnp.zeros_like(ref)


def unit(tile, k, u):
    return tile[k, :, u * N : (u + 1) * N]


def chunk_of(ref, d):
    return ref.at[d // 8, pl.ds(32 * (d % 8), 32)]


def even_first(rows, offs, beta, obj, prev, probe, amp, fwd, bwd, z0, even_low, even_high, ahead, loss):
    for u in range(2):
        for k in range(2):
            now = unit(obj, k, u)
            z0[u, k] = now + beta[0] * (now - unit(prev, k, u))
    all_positions(rows, offs, z0, probe, amp, fwd, bwd, even_low, even_high, loss)
    b = beta[1]
    for k in range(2):
        ahead[k] = (1.0 + b) * (z0[0, k] - STEP * even_low[k]) - b * unit(obj, k, 0)


def odd_first(rows, offs, z0, halo, probe, amp, fwd, bwd, odd_low, odd_high, loss, z):
    z[0] = z0[0]
    for d in range(16):
        chunk_of(z.at[1], d)[...] = halo[d]
    all_positions(rows, offs, z, probe, amp, fwd, bwd, odd_low, odd_high, loss)


def odd_second(
    rows, offs, beta, z0, obj, even_high, odd_low, odd_high, ahead, probe, amp, fwd, bwd,
    mid, low_second, high_second, loss, z,
):
    b = beta[1]
    scale = (1.0 + b) * STEP
    for k in range(2):
        now = z0[0, k] - STEP * (even_high[k] + odd_low[k])
        mid[k] = now + b * (now - obj[k])
        z[0, k] = mid[k]
    for d in range(16):
        chunk_of(z.at[1], d)[...] = ahead[d, :32] - scale * chunk_of(odd_high, d)[...]
    all_positions(rows, offs, z, probe, amp, fwd, bwd, low_second, high_second, loss)


def even_out(rows, offs, beta, ahead, from_left, mid, loss_a, loss_b, loss_c, probe, amp, fwd, start, sums, high, low, loss, z):
    @pl.when(pl.program_id(0) == 0)
    def _():
        clear(loss)
        scale = (1.0 + beta[1]) * STEP
        for d in range(16):
            chunk_of(z.at[0], d)[...] = chunk_of(ahead, d)[...] - scale * from_left[d]
        z[1] = mid[...]
        start[...] = z[0]

    weighted = way_out(rows, offs, z, probe, amp, 0, fwd, loss, pl.program_id(0) * GROUP)
    high[...] = weighted.astype(bf16)
    low[...] = (weighted - high[...].astype(f32)).astype(bf16)

    @pl.when(pl.program_id(0) == pl.num_programs(0) - 1)
    def _():
        whole = lambda x: jnp.sum(jnp.sum(x, axis=0, keepdims=True), axis=1, keepdims=True)
        lane = lax.broadcasted_iota(jnp.int32, (32, N), 1)
        line = lax.broadcasted_iota(jnp.int32, (32, N), 0)
        both = jnp.where(line < 16, whole(loss_a[...] + loss_b[...]), whole(loss_c[...] + loss[...]))
        sums[...] = jnp.where(lane == N - 1, both, 0.0)


def even_back(rows, offs, start, mid, odd_low, probe, high, low, bwd, tile, even_low, even_high):
    @pl.when(pl.program_id(0) == 0)
    def _():
        clear(even_low, even_high)

    way_back(rows, offs, probe, (high, low), bwd, even_low, even_high, pl.program_id(0) * GROUP)

    @pl.when(pl.program_id(0) == pl.num_programs(0) - 1)
    def _():
        for k in range(2):
            tile[k, :, :N] = start[k] - STEP * even_low[k]
            tile[k, :, N:] = mid[k] - STEP * (even_high[k] + odd_low[k])


def run(kernel, steps, args, outs, scratch, flops, limit=VMEM_BYTES):
    whole = lambda a: pl.BlockSpec(a.shape, lambda i, n=len(a.shape): (0,) * n)
    out_shape = [jax.ShapeDtypeStruct(s, d) for s, d, _ in outs]
    return pl.pallas_call(
        kernel,
        grid=(steps,),
        out_shape=out_shape,
        in_specs=[spec or whole(a) for a, spec in args],
        out_specs=[spec or whole(o) for o, (_, _, spec) in zip(out_shape, outs)],
        scratch_shapes=scratch,
        compiler_params=pltpu.CompilerParams(vmem_limit_bytes=limit),
        cost_estimate=pl.CostEstimate(flops=flops, bytes_accessed=2**22, transcendentals=0),
    )(*[a for a, _ in args])


def small_call(kernel, args, outs, scratch=(), limit=6 * 2**20):
    return pl.pallas_call(
        kernel,
        out_shape=[jax.ShapeDtypeStruct(s, d) for s, d, _ in outs],
        in_specs=[spec for _, spec in args],
        out_specs=[spec for _, _, spec in outs],
        scratch_shapes=list(scratch),
        compiler_params=pltpu.CompilerParams(vmem_limit_bytes=limit),
    )(*[a for a, _ in args])


def start_all(pairs, sems):
    copies = [pltpu.make_async_copy(a, b, sems.at[i]) for i, (a, b) in enumerate(pairs)]
    for c in copies:
        c.start()
    return copies


def prepare(
    owner_map, row_tops, restart, table, cols, obj, prev, amp, send, rows, inv, right, left, beta, now, before, sems
):
    band = lax.axis_index("ty")
    for c in range(16):
        inv[owner_map[band, c]] = c
    copies = start_all([(amp.at[2 * inv[d]], send.at[d, pl.ds(0, N)]) for d in range(16)], sems)
    edges = start_all([(obj.at[:, :, pl.ds(0, N)], now), (prev.at[:, :, pl.ds(0, N)], before)], sems.at[pl.ds(16, 2)])
    for c in range(16):
        owner = owner_map[band, c]
        right[owner] = owner_map[band, (c + 1) % 16]
        left[owner] = owner_map[band, (c + 15) % 16]
        rows[c] = row_tops[band * 16 + c]
    for k in range(2):
        beta[k] = (table[restart[k] - 1] - 1.0) / table[restart[k]]
    for c in edges:
        c.wait()
    now[...] = now[...] + beta[0] * (now[...] - before[...])
    lane = lax.broadcasted_iota(jnp.int32, (32, N), 1)
    line = lax.broadcasted_iota(jnp.int32, (32, N), 0)
    for d in range(16):
        col = inv[d]
        even = cols[0, 2 * col] - 2 * N * col
        odd = cols[0, 2 * col + 1] - 2 * N * col - N
        places = jnp.where(line == 0, even, odd).astype(f32)
        send[d, N:] = jnp.where(lane == N - 1, places, chunk_of(now, d)[...])
    for c in copies:
        c.wait()


def pass_halo(right, inv, got, amp, send, off_even, off_odd, places, edges, sems):
    copies = start_all([(amp.at[2 * inv[d] + 1], send.at[d, pl.ds(0, N)]) for d in range(16)], sems)
    fetch_edges = pltpu.make_async_copy(got.at[:, pl.ds(N, 32)], edges, sems.at[16])
    fetch_places = pltpu.make_async_copy(got.at[:, pl.ds(N, 2)], places, sems.at[17])
    fetch_edges.start()
    fetch_places.start()
    fetch_edges.wait()
    for d in range(16):
        send[d, N:] = edges[right[d]]
    fetch_places.wait()
    for r in range(16):
        off_even[r] = places[r, 0, N - 1].astype(jnp.int32)
        off_odd[r] = places[r, 1, N - 1].astype(jnp.int32)
    for c in copies:
        c.wait()


def pass_ahead(right, ahead, odd_high, send, edge, sem):
    fetch = pltpu.make_async_copy(odd_high, edge, sem)
    fetch.start()
    for d in range(16):
        send[d, :32] = ahead[right[d]]
    fetch.wait()
    for d in range(16):
        send[d, 32:] = chunk_of(edge, d)[...]


def pass_left(left, got, send):
    for d in range(16):
        send[d] = got[left[d], 32:]


def pass_last(left, got, sums, send):
    for d in range(16):
        send[d] = got[left[d]] + sums[...]


def finish(tile, got, out):
    edge = lax.broadcasted_iota(jnp.int32, (32, N), 1) < N - 1
    for d in range(16):
        at = pl.ds(32 * (d % 8), 32)
        out[d // 8, at] = tile[d // 8, at] - STEP * jnp.where(edge, got[d], 0.0)


def swap(block, axis="tx"):
    return lax.all_to_all(block, axis, 0, 0, tiled=True)


def shards(obj, prev, probe, amplitude, row_tops, scan_cols, restart, owner_map):
    fwd, bwd = dft_tables()
    ints = ((16,), jnp.int32, SMEM)
    unit_out, loss_out = ((2, 256, N), f32, None), ((8, N), f32, None)
    z_vmem = pltpu.VMEM((2, 2, 256, N), f32)
    unit_vmem = pltpu.VMEM((2, 256, N), f32)
    images = pl.BlockSpec((16, N, N), lambda i: (0, 0, 0))
    right_unit = pl.BlockSpec((1, 2, 256, N), lambda i: (1, 0, 0, 0))
    edge = pl.BlockSpec((16, 32, N), lambda i: (0, N // 32, 0))
    plain = lambda *arrays: [(a, None) for a in arrays]
    small = lambda *arrays: [(a, SMEM) for a in arrays]
    flops = 16 * 400_000_000

    amplitude = amplitude[0]
    send, rows, inv, right, left, beta = small_call(
        prepare,
        small(owner_map, row_tops, restart, momentum_table(), scan_cols)
        + [(obj, ANY), (prev, ANY), (amplitude, ANY)],
        [((16, N + 32, N), f32, VMEM), ints, ints, ints, ints, ((2,), f32, SMEM)],
        [unit_vmem, unit_vmem, pltpu.SemaphoreType.DMA((18,))], limit=VMEM_BYTES,
    )
    amp_even = swap(send)
    send, off_even, off_odd = small_call(
        pass_halo, small(right, inv) + [(amp_even, ANY), (amplitude, ANY)],
        [((16, N + 32, N), f32, VMEM), ints, ints],
        [pltpu.SMEM((16, 2, N), f32), pltpu.VMEM((16, 32, N), f32), pltpu.SemaphoreType.DMA((18,))], limit=VMEM_BYTES,
    )
    amp_odd = swap(send)
    z0, even_low, even_high, ahead, loss_a = run(
        even_first, 1, small(rows, off_even, beta) + plain(obj, prev, probe) + [(amp_even, images)] + plain(fwd, bwd),
        [((2, 2, 256, N), f32, None), unit_out, unit_out, unit_out, loss_out], [], flops,
    )
    got = swap(ahead.reshape(16, 32, N))
    odd_low, odd_high, loss_b = run(
        odd_first, 1,
        small(rows, off_odd) + [(z0, right_unit), (amp_odd, edge)] + plain(probe) + [(amp_odd, images)] + plain(fwd, bwd),
        [unit_out, unit_out, loss_out], [z_vmem], flops,
    )
    (send,) = small_call(
        pass_ahead, small(right) + [(got, VMEM), (odd_high, HBM)], [((16, 64, N), f32, VMEM)],
        [unit_vmem, pltpu.SemaphoreType.DMA(())],
    )
    got = swap(send)
    (send,) = small_call(pass_left, small(left) + [(got, VMEM)], [((16, 32, N), f32, VMEM)])
    from_left = swap(send)
    mid, odd_low_second, odd_high_second, loss_c = run(
        odd_second, 1,
        small(rows, off_odd, beta) + [(z0, right_unit), (obj, pl.BlockSpec((2, 256, N), lambda i: (0, 0, 1)))]
        + plain(even_high, odd_low, odd_high, got, probe)
        + [(amp_odd, images)] + plain(fwd, bwd),
        [unit_out, unit_out, unit_out, loss_out], [z_vmem], flops,
    )
    last = swap(odd_high_second.reshape(16, 32, N))
    half_block = pl.BlockSpec((GROUP * 2 * N, 2 * N), lambda i: (i, 0))
    half_out = ((16 * 2 * N, 2 * N), bf16, half_block)
    start, sums, high, low = run(
        even_out, 16 // GROUP,
        small(rows, off_even, beta) + plain(ahead, from_left, mid, loss_a, loss_b, loss_c, probe)
        + [(amp_even, pl.BlockSpec((GROUP, N, N), lambda i: (i, 0, 0)))] + plain(fwd),
        [unit_out, ((32, N), f32, None), half_out, half_out], [pltpu.VMEM((8, N), f32), z_vmem], flops // 2,
    )
    (send,) = small_call(
        pass_last, small(left) + [(last, VMEM), (sums, VMEM)], [((16, 32, N), f32, VMEM)]
    )
    got = swap(send)
    (tile,) = run(
        even_back, 16 // GROUP,
        small(rows, off_even) + plain(start, mid, odd_low_second, probe)
        + [(high, half_block), (low, half_block)] + plain(bwd),
        [((2, 256, 256), f32, None)], [unit_vmem, unit_vmem], flops // 2,
    )
    got, tile = lax.optimization_barrier((got, tile))
    sums = jnp.broadcast_to(jnp.tile(jnp.sum(got[:, :, N - 1], axis=0), 4), (8, N))
    sums = swap(sums, "ty")
    left_block = pl.BlockSpec((2, 256, N), lambda i: (0, 0, 0))
    tile = pl.pallas_call(
        finish,
        grid=(1,),
        out_shape=jax.ShapeDtypeStruct((2, 256, 256), f32),
        in_specs=[left_block, pl.BlockSpec((16, 32, N), lambda i: (0, 0, 0))],
        out_specs=left_block,
        input_output_aliases={0: 0},
        compiler_params=pltpu.CompilerParams(vmem_limit_bytes=VMEM_BYTES),
    )(tile, got)
    losses = jnp.sum(sums, axis=0)[: 32 : 16] * (0.5 / 67108864.0)
    return (tile, losses)


def solution(mesh):
    in_specs = (
        P(None, "ty", "tx"),
        P(None, "ty", "tx"),
        P(),
        P(("ty", "tx"), None, None, None),
        P(),
        P(("ty", "tx"), None),
        P(),
        P(),
    )
    return jax.shard_map(
        shards, mesh=mesh, in_specs=in_specs, out_specs=(P(None, "ty", "tx"), P()), check_vma=False
    )
```
